128 devices in a mesh: fsdp: 128 (over z, y, x, core).
Axes of the slice: x: 4, y: 4, z: 4, core: 2. Of those that a mesh axis runs over, the one named last changes fastest.
Arguments:
- inputs: bfloat16 [2, 128, 128, 1024], P(None, 'fsdp'), may hold values from -6 to 6
- cotangent: bfloat16 [2, 128, 128, 1024], P(None, 'fsdp'), may hold values from -6 to 6
- segments: int32 [2, 128, 128], P(None, 'fsdp'), may hold values from 0 to 3, never falling along the last dimension, each value on 1 to 64 neighbouring positions
- positions: int32 [2, 128, 128], P(None, 'fsdp'), may hold values from 0 to 4095, as said below
- attention_weight: float32 [1024, 2048], P('fsdp'), may hold values from -0.1875 to 0.1875
- output_weight: float32 [1024, 1024], P('fsdp'), may hold values from -0.75 to 0.75
- joint_projection_matrix: float32 [1024, 9216], P('fsdp'), may hold values from -0.1875 to 0.1875
- down_weight: float32 [4608, 1024], P('fsdp'), may hold values from -0.09375 to 0.09375
- gains: float32 [2176], P('fsdp'), may hold values from 0.37 to 3.33
- first_attend: float32 [1024, 2048], P('fsdp'), may hold values from -7 to 7
- first_output: float32 [1024, 1024], P('fsdp'), may hold values from -0.75 to 0.75
- first_gate_up: float32 [1024, 9216], P('fsdp'), may hold values from -0.75 to 0.75
- first_down: float32 [4608, 1024], P('fsdp'), may hold values from -1.5 to 1.5
- first_gains: float32 [2176], P('fsdp'), may hold values from -6 to 6
- second_attend: float32 [1024, 2048], P('fsdp'), may hold values from 4.9152 to 19.6608
- second_output: float32 [1024, 1024], P('fsdp'), may hold values from 0.0688128 to 0.278528
- second_gate_up: float32 [1024, 9216], P('fsdp'), may hold values from 0.0557056 to 0.229376
- second_down: float32 [4608, 1024], P('fsdp'), may hold values from 0.262144 to 1.114112
- second_gains: float32 [2176], P('fsdp'), may hold values from 4.096 to 16.384
Outputs:
- result: bfloat16 [2, 128, 128, 1024], P(None, 'fsdp')
- grad_inputs: float32 [2, 128, 128, 1024], P(None, 'fsdp')
- grad_norm: float32 [], replicated
- new_attend: float32 [1024, 2048], P('fsdp')
- new_output: float32 [1024, 1024], P('fsdp')
- new_gate_up: float32 [1024, 9216], P('fsdp')
- new_down: float32 [4608, 1024], P('fsdp')
- new_gains: float32 [2176], P('fsdp')
- new_first_attend: float32 [1024, 2048], P('fsdp')
- new_first_output: float32 [1024, 1024], P('fsdp')
- new_first_gate_up: float32 [1024, 9216], P('fsdp')
- fresh_mean_shrink_matrix: float32 [4608, 1024], P('fsdp')
- new_first_gains: float32 [2176], P('fsdp')
- new_second_attend: float32 [1024, 2048], P('fsdp')
- new_second_output: float32 [1024, 1024], P('fsdp')
- new_second_gate_up: float32 [1024, 9216], P('fsdp')
- new_second_down: float32 [4608, 1024], P('fsdp')
- new_second_gains: float32 [2176], P('fsdp')
The draws below stay inside these ranges and needn't reach their ends.
Inputs may be any that keep to these rules, and one draw needn't show every extreme that they name: `segments`: along each sequence the numbers never fall; each of the 4 documents holds 1 to 64 tokens. Along each sequence the positions rise by one from token to token.
All inputs are finite; a program needn't handle non-finite values.
Results may differ from the reference program's by a relative error of at most 0.015.
The reference program's roundings to bfloat16 on the way count: a program that leaves them out, or rounds other values in their place, can miss the bound.
Values may be sent and summed in bfloat16 or wider, within the bound.
A program may use at most 256 MiB of HBM per device.

```python
import math
import jax
import jax.numpy as jnp
import numpy as np
from jax import lax

D = 1024
H = 16
KV = 8
HD = 64
FF = 4608
SEQ = 128
MICRO = 2
DOCS = 4
MAXPOS = 4096
STEP = 10
SEQS = 128
QKV = 2048
NGAIN = 2176
NPARAM = 17303680


def draw_positions(key, part):
    key = jax.random.fold_in(key, 23)
    key_starts, key_pick = jax.random.split(key)
    count = MICRO * SEQS
    starts = jax.random.randint(key_starts, (count,), 0, MAXPOS - SEQ + 1)
    chosen = jax.random.randint(key_pick, (), 0, count)
    order = jnp.arange(count)
    starts = jnp.where(order == chosen, MAXPOS - SEQ, starts)
    starts = jnp.where(order == (chosen + 1) % count, 0, starts)
    placed = starts[:, None] + jnp.arange(SEQ)[None, :]
    return placed.reshape(MICRO, SEQS, SEQ).astype(jnp.int32)


def draw_gains(key, part):
    key = jax.random.fold_in(key, 11)
    key_rough, key_heads = jax.random.split(key)
    spot = (jnp.arange(2 * D) % D).astype(jnp.float32) / D
    rising = 0.6 * 3.0 ** spot
    rough = jax.random.uniform(key_rough, (2 * D,), jnp.float32, 0.75, 1.33)
    head_gains = jax.random.uniform(key_heads, (2 * HD,), jnp.float32, 1.0, 1.6)
    return jnp.concatenate([rising * rough, head_gains]).astype(jnp.float32)


def block_scale(own_key, shape, shards, smallest, top_value):
    factor_of = 1.0
    for dim, blocks in shards:
        heights = jax.random.uniform(jax.random.fold_in(jax.random.fold_in(own_key, 6), dim), (blocks,), jnp.float32, smallest / len(shards), top_value / len(shards))
        factor_of = factor_of * jnp.repeat(jnp.exp(heights), shape[dim] // blocks).reshape((-1,) + (1,) * (len(shape) - 1 - dim))
    return factor_of


def profile(amount, total, limit, skew):
    loads = [(1 << 20) // math.isqrt(rank ** skew) + 1 for rank in range(2, amount + 1)]
    spare, given = total - limit - (amount - 1), [1] * (amount - 1)
    while spare > 0:
        movable = [i for i in range(amount - 1) if given[i] < limit]
        mass, remaining = sum([loads[i] for i in movable]), spare
        for i in movable:
            extra = min(limit - given[i], max(1, remaining * loads[i] // mass), spare)
            given[i] = given[i] + extra
            spare = spare - extra
    return np.array([limit] + given)


def ragged(own_key, count, total, bound, skew):
    if count == 2:
        one = jax.random.randint(own_key, (), max(1, total - bound), min(bound, total - 1) + 1)
        return jnp.stack([one, total - one])
    lengths = jnp.asarray(profile(count, total, bound, skew), jnp.int32)
    couples = (count - 1) // 2
    source_of, receiver = lengths[1:1 + 2 * couples:2], lengths[2:2 + 2 * couples:2]
    room = jnp.minimum(source_of - 1, bound - receiver)
    passed = jax.random.randint(jax.random.fold_in(own_key, 1), (couples,), 0, 1 << 20) % (room + 1)
    lengths = lengths.at[1:1 + 2 * couples:2].set(source_of - passed).at[2:2 + 2 * couples:2].set(receiver + passed)
    return lengths[jax.random.permutation(jax.random.fold_in(own_key, 2), count)]


def normal_values(stream_key, shape, scale, limit, cuts=(), kind=jnp.bfloat16):
    factor_of = block_scale(stream_key, shape, cuts, -0.22, 0.18) if cuts else 1.0
    array = jax.random.normal(stream_key, shape, jnp.float32) * scale * factor_of
    return jnp.minimum(jnp.maximum(array, -limit), limit).astype(kind)


def setup_inputs(seed: int = 0) -> dict:
    keys = jax.random.split(jax.random.key(seed), 20)
    return {
        "inputs": normal_values(keys[0], (MICRO, SEQS, SEQ, D), 1.0, 6.0, ((1, 128),)),
        "cotangent": normal_values(keys[1], (MICRO, SEQS, SEQ, D), 1.0, 6.0, ((1, 128),)),
        "segments": jax.vmap(lambda own: jnp.searchsorted(jnp.cumsum(ragged(own, DOCS, SEQ, SEQ // 2, 0)), jnp.arange(SEQ), side="right"))(jax.random.split(keys[2], MICRO * SEQS)).reshape((MICRO, SEQS, SEQ)).astype(jnp.int32),
        "positions": draw_positions(jax.random.fold_in(keys[19], 71), 0),
        "attention_weight": normal_values(keys[4], (D, QKV), D ** -0.5, 0.1875, ((0, 128),), jnp.float32),
        "output_weight": normal_values(keys[5], (H * HD, D), (H * HD // 16) ** -0.5, 0.75, ((0, 128),), jnp.float32),
        "joint_projection_matrix": normal_values(keys[6], (D, 2 * FF), D ** -0.5, 0.1875, ((0, 128),), jnp.float32),
        "down_weight": normal_values(keys[7], (FF, D), FF ** -0.5, 0.09375, ((0, 128),), jnp.float32),
        "gains": draw_gains(jax.random.fold_in(keys[19], 71), 0),
        "first_attend": normal_values(keys[9], (D, QKV), (0.006 * (MICRO * SEQS * SEQ) ** 0.5), 7.0, ((0, 128),), jnp.float32),
        "first_output": normal_values(keys[10], (H * HD, D), (0.0007 * (MICRO * SEQS * SEQ) ** 0.5), 0.75, ((0, 128),), jnp.float32),
        "first_gate_up": normal_values(keys[11], (D, 2 * FF), (0.00064 * (MICRO * SEQS * SEQ) ** 0.5), 0.75, ((0, 128),), jnp.float32),
        "first_down": normal_values(keys[12], (FF, D), (0.0014 * (MICRO * SEQS * SEQ) ** 0.5), 1.5, ((0, 128),), jnp.float32),
        "first_gains": normal_values(keys[13], (NGAIN,), (0.0055 * (MICRO * SEQS * SEQ) ** 0.5), 6.0, ((0, 128),), jnp.float32),
        "second_attend": jnp.clip(jnp.exp(math.log(19.6608) - 1.3862944 * jax.random.uniform(keys[14], (D, QKV), jnp.float32) ** block_scale(keys[14], (D, QKV), ((0, 128),), -0.2, 0.2)), 4.9152, 19.6608),
        "second_output": jnp.clip(jnp.exp(math.log(0.278528) - 1.3981288 * jax.random.uniform(keys[15], (H * HD, D), jnp.float32) ** block_scale(keys[15], (H * HD, D), ((0, 128),), -0.2, 0.2)), 0.0688128, 0.278528),
        "second_gate_up": jnp.clip(jnp.exp(math.log(0.229376) - 1.4152819 * jax.random.uniform(keys[16], (D, 2 * FF), jnp.float32) ** block_scale(keys[16], (D, 2 * FF), ((0, 128),), -0.2, 0.2)), 0.0557056, 0.229376),
        "second_down": jnp.clip(jnp.exp(math.log(1.114112) - 1.446919 * jax.random.uniform(keys[17], (FF, D), jnp.float32) ** block_scale(keys[17], (FF, D), ((0, 128),), -0.2, 0.2)), 0.262144, 1.114112),
        "second_gains": jnp.clip(jnp.exp(math.log(16.384) - 1.3862944 * jax.random.uniform(keys[18], (NGAIN,), jnp.float32) ** block_scale(keys[18], (NGAIN,), ((0, 128),), -0.2, 0.2)), 4.096, 16.384),
    }


EPS = 1e-05
THETA = 1000000.0
CLIP_COEF = 0.02
BETA_ONE = 0.9
SQUARE_DAMPING = 0.95
MOMENT_FLOOR = 1e-08
DECAY = 0.1
GAIN_RATE = 0.3
BLOCKED = -1e+30

@jax.custom_vjp
def low(v):
    return lax.optimization_barrier(v.astype(jnp.bfloat16)).astype(jnp.float32)

@jax.custom_vjp
def reduced_backward(v):
    return v

def low_keep(v):
    return (low(v), None)

def low_pass(kept, grad):
    return (grad,)

def back_keep(v):
    return (v, None)

def back_low(kept, grad):
    return (low(grad),)
low.defvjp(low_keep, low_pass)
reduced_backward.defvjp(back_keep, back_low)

def gated_product(form, left, right):
    return jnp.einsum(form, left, right, precision=lax.Precision.HIGHEST)

def norm_rows(matrix, gain):
    return matrix * lax.rsqrt(lax.optimization_barrier(jnp.mean(matrix * matrix, axis=-1, keepdims=True)) + EPS) * gain

def angles(positions_in, width):
    half_width = width // 2
    frequency = THETA ** (-jnp.arange(half_width, dtype=jnp.float32) * 2.0 / width)
    phases = positions_in.astype(jnp.float32)[..., None, None] * frequency
    return (jnp.cos(phases), jnp.sin(phases))

def rotate(matrix, cosines, sine_values):
    half_width = matrix.shape[-1] // 2
    first_half = matrix[..., :half_width]
    second_half = matrix[..., half_width:]
    return jnp.concatenate([first_half * cosines - second_half * sine_values, second_half * cosines + first_half * sine_values], axis=-1)

def counted(segment_ids):
    extent = segment_ids.shape[-1]
    order = jnp.arange(extent)
    earlier = order[:, None] >= order[None, :]
    same_doc = segment_ids[:, :, None] == segment_ids[:, None, :]
    return (same_doc & earlier)[:, None, None]

def forward(residual_state, attention_weight, output_weight, joint_projection_matrix, down_weight, gains, segment_ids, places):
    attention_weight = low(attention_weight)
    output_weight = low(output_weight)
    joint_projection_matrix = low(joint_projection_matrix)
    down_weight = low(down_weight)
    gains = low(gains)
    sequences, extent = (residual_state.shape[0], residual_state.shape[1])
    gain_attn = gains[:D]
    gain_ffn = gains[D:2 * D]
    gain_query = gains[2 * D:2 * D + HD]
    gain_keys = gains[2 * D + HD:]
    scaled_input = low(norm_rows(residual_state, gain_attn))
    mixed_rows = reduced_backward(gated_product('kbj,jv->kbv', scaled_input, attention_weight))
    query_raw = mixed_rows[..., :H * HD].reshape(sequences, extent, H, HD)
    key_raw = mixed_rows[..., H * HD:(H + KV) * HD].reshape(sequences, extent, KV, HD)
    values = low(mixed_rows[..., (H + KV) * HD:].reshape(sequences, extent, KV, HD))
    cosines, sine_values = angles(places, HD)
    queries = low(rotate(norm_rows(query_raw, gain_query), cosines, sine_values)).reshape(sequences, extent, KV, H // KV, HD)
    key_heads = low(rotate(norm_rows(key_raw, gain_keys), cosines, sine_values))
    scores = reduced_backward(gated_product('slkgh,smkh->skglm', queries, key_heads) * HD ** (-0.5))
    masked = jnp.where(counted(segment_ids), scores, BLOCKED)
    row_max = lax.optimization_barrier(jnp.max(masked, axis=-1, keepdims=True))
    raised = jnp.exp(masked - row_max)
    soft_weights = low(raised / lax.optimization_barrier(jnp.sum(raised, axis=-1, keepdims=True)))
    attention_result = gated_product('skglm,smkh->slkgh', soft_weights, values).reshape(sequences, extent, H * HD)
    attention_result = low(reduced_backward(attention_result))
    middle_rows = residual_state + reduced_backward(gated_product('vwg,gn->vwn', attention_result, output_weight))
    scaled_middle = low(norm_rows(middle_rows, gain_ffn))
    gate_up_values = reduced_backward(gated_product('tcv,vg->tcg', scaled_middle, joint_projection_matrix))
    hidden_rows = low(jax.nn.silu(gate_up_values[..., :FF]) * gate_up_values[..., FF:])
    return middle_rows + reduced_backward(gated_product('twm,mx->twx', hidden_rows, down_weight))

def adam_update(weight, first, second, gradient, rate, decay):
    new_first = BETA_ONE * first + (1.0 - BETA_ONE) * gradient
    new_second = SQUARE_DAMPING * second + (1.0 - SQUARE_DAMPING) * gradient * gradient
    corrected = new_first / (1.0 - BETA_ONE ** STEP)
    divisor = jnp.sqrt(new_second / (1.0 - SQUARE_DAMPING ** STEP)) + MOMENT_FLOOR
    return (weight - rate * (corrected / divisor + decay * weight), new_first, new_second)

def reference(inputs, cotangent, segments, positions, attention_weight, output_weight, joint_projection_matrix, down_weight, gains, first_attend, first_output, first_gate_up, first_down, first_gains, second_attend, second_output, second_gate_up, second_down, second_gains):
    params = (attention_weight, output_weight, joint_projection_matrix, down_weight, gains)
    count = MICRO * SEQS
    group = math.gcd(count, 32)
    shaped = (count // group, group, SEQ)
    stream_all = inputs.astype(jnp.float32).reshape(shaped + (D,))
    back_all = cotangent.astype(jnp.float32).reshape(shaped + (D,))
    seg_blocks = segments.reshape(shaped)
    pos_blocks = positions.reshape(shaped)

    def one_group(running_sums, batch_item):
        tokens_in, grad_out, segment_ids, places = batch_item

        def run(stream_in, *weights):
            return forward(stream_in, *weights, segment_ids, places)
        outputs, pullback = jax.vjp(run, tokens_in, *params)
        gradients = pullback(grad_out)
        running_sums = tuple((older + newer for older, newer in zip(running_sums, gradients[1:])))
        return (running_sums, (outputs.astype(jnp.bfloat16), gradients[0]))
    zero_sums = tuple((jnp.zeros_like(weight) for weight in params))
    running_sums, (outputs, grad_rows) = lax.scan(one_group, zero_sums, (stream_all, back_all, seg_blocks, pos_blocks))
    squares = sum((jnp.sum(gradient_part * gradient_part) for gradient_part in running_sums))
    grad_norm = jnp.sqrt(squares)
    clip_limit = CLIP_COEF * math.sqrt(MICRO * SEQS * SEQ * NPARAM)
    factor = clip_limit / jnp.maximum(grad_norm, clip_limit)
    step_rates = (0.8 / math.sqrt(D), 0.8 / math.sqrt(H * HD // 16), 0.8 / math.sqrt(D), 0.8 / math.sqrt(FF), GAIN_RATE)
    decays = (DECAY, DECAY, DECAY, DECAY, 0.0)
    firsts = (first_attend, first_output, first_gate_up, first_down, first_gains)
    seconds = (second_attend, second_output, second_gate_up, second_down, second_gains)
    updated = [adam_update(params[slot_index], firsts[slot_index], seconds[slot_index], running_sums[slot_index] * factor, step_rates[slot_index], decays[slot_index]) for slot_index in range(5)]
    result = outputs.reshape(MICRO, SEQS, SEQ, D)
    grad_inputs = grad_rows.reshape(MICRO, SEQS, SEQ, D)
    return (result, grad_inputs, grad_norm, updated[0][0], updated[1][0], updated[2][0], updated[3][0], updated[4][0], updated[0][1], updated[1][1], updated[2][1], updated[3][1], updated[4][1], updated[0][2], updated[1][2], updated[2][2], updated[3][2], updated[4][2])
```

```python
import functools
import math

import jax
import jax.numpy as jnp
from jax import lax
from jax.experimental import pallas as pl
from jax.experimental.pallas import tpu as pltpu
from jax.sharding import PartitionSpec as P

D = 1024
H = 16
KV = 8
HD = 64
FF = 4608
STEP = 10


EPS = 1e-05
THETA = 1000000.0
CLIP_COEF = 0.02
BETA_ONE = 0.9
SQUARE_DAMPING = 0.95
MOMENT_FLOOR = 1e-08
DECAY = 0.1
GAIN_RATE = 0.3
BLOCKED = -1e30
GATHER_COPIES = 336
SCATTER_COPIES = 176
FETCHED = 16


def counted(segments):
    wide = jnp.broadcast_to(segments.astype(jnp.float32), (128, 128))
    row = lax.broadcasted_iota(jnp.int32, (128, 128), 0)
    col = lax.broadcasted_iota(jnp.int32, (128, 128), 1)
    allowed = (wide == wide.T) & (col <= row)
    return jnp.concatenate([allowed, allowed], axis=0)


MESH = pl.DeviceIdType.MESH
HALF_ATT, HALF_OUT, HALF_JOINT, HALF_DOWN = 1024, 512, FF, 512
CUT = 1152
LAST = FF - 2 * CUT
DOWN_ROWS = FF // 128


class Place:
    def __init__(self):
        me = lax.axis_index("fsdp")
        self.core = lax.rem(me, 2)
        self.x = lax.rem(lax.div(me, 2), 4)
        self.y = lax.rem(lax.div(me, 8), 4)
        self.z = lax.div(me, 32)
        self.sibling = self.at(core=1 - self.core)

    def at(self, z=None, y=None, x=None, core=None):
        z = self.z if z is None else z
        y = self.y if y is None else y
        x = self.x if x is None else x
        core = self.core if core is None else core
        return ((z * 4 + y) * 4 + x) * 2 + core

    def near(self, axis, step):
        spot = lax.rem(getattr(self, axis) + step + 4, 4)
        return spot, self.at(**{axis: spot})

    def greet(self):
        barrier = pltpu.get_barrier_semaphore()
        others = [self.sibling]
        for step in (1, 2, 3):
            spot, device = self.near("x", step)
            others += [device, self.at(x=spot, core=1 - self.core)]
            others += [self.near("y", step)[1], self.near("z", step)[1]]
        for device in others:
            pl.semaphore_signal(barrier, inc=1, device_id=(device,), device_id_type=MESH)
        pl.semaphore_wait(barrier, len(others))


class Links:
    def __init__(self, send_sems, recv_sems):
        self.send_sems, self.recv_sems = send_sems, recv_sems
        self.copies, self.gone = [], []

    def send(self, source, target, device):
        slot = len(self.copies)
        copy = pltpu.make_async_remote_copy(
            src_ref=source,
            dst_ref=target,
            send_sem=self.send_sems.at[slot],
            recv_sem=self.recv_sems.at[slot],
            device_id=(device,),
            device_id_type=MESH,
        )
        copy.start()
        self.copies.append(copy)
        return copy

    def finish(self):
        assert len(self.copies) <= self.send_sems.shape[0]
        for copy in self.copies:
            if not any((copy is done for done in self.gone)):
                copy.wait_send()


def lanes(core, half, low, width):
    return pl.ds(pl.multiple_of(core * half + low, 128), width)


ALL = slice(None)


def near_rows(left, right):
    return lax.dot_general(left, right, (((1,), (1,)), ((), ())), preferred_element_type=jnp.float32)


def over_rows(left, right):
    return lax.dot_general(left, right, (((0,), (0,)), ((), ())), preferred_element_type=jnp.float32)


def plain(left, right):
    return lax.dot_general(left, right, (((1,), (0,)), ((), ())), preferred_element_type=jnp.float32)


def head_mean(values):
    row = lax.broadcasted_iota(jnp.int32, (128, 128), 0) < HD
    col = lax.broadcasted_iota(jnp.int32, (128, 128), 1) < HD
    same = jnp.where(row == col, 1.0, 0.0)
    sums = lax.dot_general(
        values, same, (((1,), (0,)), ((), ())),
        precision=lax.Precision.HIGHEST, preferred_element_type=jnp.float32,
    )
    return sums * (1.0 / HD)


def partner(values):
    lane = lax.broadcasted_iota(jnp.int32, values.shape, 1)
    return jnp.where(
        lax.rem(lane, HD) < HD // 2, pltpu.roll(values, 128 - HD // 2, 1), pltpu.roll(values, HD // 2, 1)
    )


def left_lanes():
    return lax.broadcasted_iota(jnp.int32, (128, 128), 1) < HD


def both(block):
    block = block.astype(jnp.float32)
    turned = pltpu.roll(block, HD, 1)
    return (
        jnp.where(left_lanes(), block, turned).astype(jnp.bfloat16),
        jnp.where(left_lanes(), turned, block).astype(jnp.bfloat16),
    )


def stacked(block):
    block = block.astype(jnp.float32)
    return jnp.concatenate(
        [jnp.where(left_lanes(), block, 0.0), jnp.where(left_lanes(), 0.0, block)], axis=0
    ).astype(jnp.bfloat16)


def attention_heads(
    raw, cosine, signed_sine, segments, gain_query, gain_key, query, key, value, attended
):
    wide, low = jnp.float32, jnp.bfloat16
    turned = []
    for block in range(12):
        mixed = raw[:, block * 128 : block * 128 + 128]
        gain = gain_query if block < 8 else gain_key
        hat = mixed * lax.rsqrt(head_mean(mixed * mixed) + EPS) * gain[...]
        turned.append((hat * cosine[...] + partner(hat) * signed_sine[...]).astype(low))
        if block % 4 == 3:
            target, start = (query, block - 3) if block < 8 else (key, 0)
            for spot, piece in enumerate(turned):
                target[:, (start + spot) * 128 : (start + spot) * 128 + 128] = piece
            turned = []
    value[...] = raw[:, (H + KV) * HD :].astype(low)
    counts = []
    for sequence in range(2):
        counts.append(counted(segments[sequence : sequence + 1, :]))

    @pl.loop(0, 4)
    def _(pair):
        pair_cols = pl.ds(pl.multiple_of(pair * 128, 128), 128)
        cols = [pl.ds(pl.multiple_of(pair * 256 + parity * 128, 128), 128) for parity in range(2)]
        units = []
        for sequence in range(2):
            rows = slice(sequence * 128, sequence * 128 + 128)
            keys, values = both(key[rows, pair_cols]), both(value[rows, pair_cols])
            for parity in range(2):
                units.append(
                    (sequence, rows, cols[parity], stacked(query[rows, cols[parity]]), keys[parity], values[parity])
                )
        scores = [
            jnp.where(counts[unit[0]], near_rows(unit[3], unit[4]) * HD ** (-0.5), BLOCKED) for unit in units
        ]
        raised = [jnp.exp(score - jnp.max(score, axis=1, keepdims=True)) for score in scores]
        soft = [(rise / jnp.sum(rise, axis=1, keepdims=True)).astype(low) for rise in raised]
        parts = [plain(weights, unit[5]) for weights, unit in zip(soft, units)]
        for unit, part in zip(units, parts):
            attended[unit[1], unit[2]] = jnp.where(left_lanes(), part[0:128], part[128:256]).astype(low)


def attention_heads_back(
    grad_att, raw, query, key, value, cosine, signed_sine, segments, gain_query, gain_key,
    grad_mixed, head_gains, grad_query, grad_key,
):
    wide, low = jnp.float32, jnp.bfloat16
    counts = []
    for sequence in range(2):
        counts.append(counted(segments[sequence : sequence + 1, :]))

    @pl.loop(0, 4)
    def _(pair):
        pair_cols = pl.ds(pl.multiple_of(pair * 128, 128), 128)
        cols = [pl.ds(pl.multiple_of(pair * 256 + parity * 128, 128), 128) for parity in range(2)]
        units = []
        for sequence in range(2):
            rows = slice(sequence * 128, sequence * 128 + 128)
            keys, values = both(key[rows, pair_cols]), both(value[rows, pair_cols])
            for parity in range(2):
                units.append(
                    (
                        counts[sequence],
                        stacked(query[rows, cols[parity]]),
                        stacked(grad_att[rows, cols[parity]]),
                        keys[parity],
                        values[parity],
                    )
                )
        scores = [
            jnp.where(count, near_rows(queries, keys) * HD ** (-0.5), BLOCKED)
            for count, queries, _, keys, _ in units
        ]
        raised = [jnp.exp(score - jnp.max(score, axis=1, keepdims=True)) for score in scores]
        soft = [rise / jnp.sum(rise, axis=1, keepdims=True) for rise in raised]
        grad_soft = [near_rows(grads, values) for _, _, grads, _, values in units]
        grad_scores = [
            (weights * (grad - jnp.sum(grad * weights, axis=1, keepdims=True))).astype(low)
            for weights, grad in zip(soft, grad_soft)
        ]
        value_parts = [over_rows(weights.astype(low), unit[2]) for weights, unit in zip(soft, units)]
        key_parts = [over_rows(grad, unit[1]) * HD ** (-0.5) for grad, unit in zip(grad_scores, units)]
        query_parts = [plain(grad, unit[3]) * HD ** (-0.5) for grad, unit in zip(grad_scores, units)]
        value_parts = [part + pltpu.roll(part, HD, 1) for part in value_parts]
        key_parts = [part + pltpu.roll(part, HD, 1) for part in key_parts]
        value_cols = pl.ds(pl.multiple_of((H + KV) * HD + pair * 128, 128), 128)
        for sequence in range(2):
            rows = slice(sequence * 128, sequence * 128 + 128)
            even, odd = 2 * sequence, 2 * sequence + 1
            for spot, unit in enumerate((even, odd)):
                part = query_parts[unit]
                grad_query[rows, cols[spot]] = jnp.where(left_lanes(), part[0:128], part[128:256])
            grad_key[rows, pair_cols] = jnp.where(left_lanes(), key_parts[even], key_parts[odd])
            grad_mixed[rows, value_cols] = jnp.where(
                left_lanes(), value_parts[even], value_parts[odd]
            ).astype(low)

    gains = []
    for block in range(12):
        source, spot, gain = (grad_query, block, gain_query) if block < 8 else (grad_key, block - 8, gain_key)
        grad = source[:, spot * 128 : spot * 128 + 128]
        grad = grad * cosine[...] - partner(grad) * signed_sine[...]
        mixed = raw[:, block * 128 : block * 128 + 128]
        inverse = lax.rsqrt(head_mean(mixed * mixed) + EPS)
        hat = mixed * inverse
        gains.append(jnp.sum(grad * hat, axis=0, keepdims=True))
        grad = grad * gain[...]
        grad_mixed[:, block * 128 : block * 128 + 128] = (
            inverse * (grad - hat * head_mean(grad * hat))
        ).astype(low)
    head_gains[0:1, :] = sum(gains[1:8], gains[0])
    head_gains[1:2, :] = sum(gains[9:12], gains[8])


def gather_kernel(
    att, out, joint, down, gains, tokens, cotangent, cosine, signed_sine, segments,
    kept_att, kept_out, hidden_pair, joint_pair, norm_pair, attended_pair, mid_pair, down_pair,
    raw_out, query_out, key_out, value_out,
    result, grad_middle, ffn_gains, gain_attn, gain_query, gain_key,
    raw, query, key, value, full_att, full_out, full_joint, full_down,
    got_att, got_out, got_joint, low_att, low_out, low_joint,
    pad_down, send_down, got_down, rows_down, low_down,
    core_gains, x_gains, all_gains, gain_ffn, pad_gains,
    norm, attended, mid, norm_t, attended_t, mid_t, middle, middle_sum, grad_mid,
    gate, up, grad_hidden, hidden, hidden_t, grad_joint,
    send_sems, recv_sems, own_sems,
):
    place = Place()
    core, z, y, x = place.core, place.z, place.y, place.x
    wide, low = jnp.float32, jnp.bfloat16
    links = Links(send_sems, recv_sems)
    place.greet()
    other = 1 - core
    seat = 2 * x + core
    locals_ = []

    def keep(source, target):
        copy = pltpu.make_async_copy(source, target, own_sems.at[len(locals_)])
        copy.start()
        locals_.append(copy)
        return copy

    swaps = []
    for source, target, half in (
        (att, got_att, HALF_ATT), (out, got_out, HALF_OUT), (joint, got_joint, HALF_JOINT)
    ):
        swaps.append(links.send(source.at[:, lanes(other, half, 0, half)], target, place.sibling))
    row = lax.broadcasted_iota(jnp.int32, (8, 128), 0)
    pad_gains[...] = jnp.zeros_like(pad_gains)
    pad_gains[:, 0:17] = gains[...]
    core_gains[core] = jnp.where(row == seat, pad_gains[...], 0.0)
    gain_swap = links.send(core_gains.at[core], core_gains.at[core], place.sibling)
    pad_down[...] = jnp.zeros_like(pad_down)
    pad_down[0:DOWN_ROWS, :] = down[...]
    for part in range(2):
        send_down[part] = pad_down[:, part * 512 : part * 512 + 512].astype(low)
    down_moves = []
    for step in range(4):
        spot = lax.rem(x + step, 4)
        for flip in range(2):
            if step or flip:
                target_core = lax.rem(core + flip, 2)
                down_moves.append(
                    links.send(
                        send_down.at[target_core], got_down.at[seat], place.at(x=spot, core=target_core)
                    )
                )
    got_down[pl.ds(seat, 1)] = send_down[pl.ds(core, 1)]
    own_copies = []
    for copy, source, target, chip, full, half in (
        (swaps[0], att, got_att, low_att, full_att, HALF_ATT),
        (swaps[1], out, got_out, low_out, full_out, HALF_OUT),
        (swaps[2], joint, got_joint, low_joint, full_joint, HALF_JOINT),
    ):
        copy.wait_recv()
        for begin in range(0, half, 512):
            own = source[:, lanes(core, half, begin, 512)]
            got = target[:, begin : begin + 512]
            first = jnp.where(core == 0, own, got)
            second = jnp.where(core == 0, got, own)
            chip[:, begin : begin + 512] = jnp.concatenate([first, second], axis=0).astype(low)
        own_copies.append(keep(chip, full.at[z, y, x, :, lanes(core, half, 0, half)]))

    att_a = (full_att, HALF_ATT, 0, 512, 4)
    att_b = (full_att, HALF_ATT, 512, 512, 4)
    out_c = (full_out, HALF_OUT, 0, 512, 4)
    down_a = (full_down, HALF_DOWN, 0, 256, 18)
    down_b = (full_down, HALF_DOWN, 256, 256, 18)
    joint_first = (full_joint, HALF_JOINT, 0, 1152, 4)
    joint_rest = [
        [(full_joint, HALF_JOINT, 1152 * turn + 384 * third, 384, 4) for third in range(3)]
        for turn in range(1, 4)
    ]

    def shape(array, zs, ys, xs):
        ref, half, begin, width, _ = array
        return ref.at[zs, ys, xs, :, lanes(core, half, begin, width)]

    def direct(source, array, axis):
        return [
            links.send(source, shape(array, z, y, x), place.near(axis, step)[1]) for step in (1, 3, 2)
        ]

    first = direct(low_att.at[:, 0:512], att_a, "x")
    first += direct(low_att.at[:, 512:1024], att_b, "x")
    first += direct(low_out, out_c, "y")
    first += direct(low_joint.at[:, 0:1152], joint_first, "y")
    for arrays in joint_rest:
        for array, axis in zip(arrays, "xxy"):
            first += direct(low_joint.at[:, array[2] : array[2] + 384], array, axis)
    gain_swap.wait_recv()
    x_gains[x] = core_gains[0] + core_gains[1]
    gain_moves = [
        links.send(x_gains.at[x], x_gains.at[x], place.near("x", step)[1]) for step in (1, 2, 3)
    ]
    for move in down_moves:
        move.wait_recv()
    for spot in range(8):
        rows_down[spot * DOWN_ROWS : spot * DOWN_ROWS + DOWN_ROWS, :] = got_down[spot].astype(wide)[
            0:DOWN_ROWS
        ]
    low_down[...] = rows_down[...].reshape(18, 16, 512).astype(low)
    own_copies.append(keep(low_down, full_down.at[z, y, :, :, lanes(core, 512, 0, 512)]))
    for move in gain_moves:
        move.wait_recv()
    all_gains[z, y] = x_gains[0] + x_gains[1] + x_gains[2] + x_gains[3]
    gain_moves = [
        links.send(all_gains.at[z, y], all_gains.at[z, y], place.near("y", step)[1])
        for step in (1, 2, 3)
    ]
    keep(cotangent.at[:, lanes(core, 512, 0, 512)], down_pair.at[0])
    pair_moves = [
        links.send(cotangent.at[:, lanes(other, 512, 0, 512)], down_pair.at[1], place.sibling)
    ]
    for copy in own_copies:
        copy.wait()
    for move in first:
        move.wait_recv()

    def slab_zy(array, spot, half):
        return shape(array, z, spot, half)

    def slab_yz(array, spot, half):
        return shape(array, spot, y, half)

    def slab_xz(array, spot, half):
        return shape(array, spot, half, x)

    def slab_z(array, spot, half):
        return shape(array, spot, half, ALL)

    def slab_y(array, spot, half):
        return shape(array, half, spot, ALL)

    def slab_x(array, spot, half):
        return shape(array, half, ALL, spot)

    def plans(arrays):
        ones = ((slab_zy, "y", True), (slab_yz, "z", True), (slab_xz, "z", False))
        twos = ((slab_z, "z", False), (slab_y, "y", False), (slab_x, "x", False))
        return (
            [(array,) + one for array, one in zip(arrays, ones)],
            [(array,) + two for array, two in zip(arrays, twos)],
        )

    stages = [plans(arrays) for arrays in [(att_a, att_b, out_c), (down_a, down_b, joint_first)] + joint_rest]

    def halves(inner, array):
        size = array[4] // 2 if inner else 2
        return pl.ds(0, size), pl.ds(size, size)

    def hand_over(ref, handed):
        handed.append(links.send(ref, ref, place.sibling))

    def ring_start(plans):
        moves = []
        for array, slab, axis, inner in plans:
            held = slab(array, getattr(place, axis), ALL)
            moves.append(
                [links.send(held, held, place.near(axis, 1)[1]), links.send(held, held, place.near(axis, -1)[1])]
            )
        return moves

    def ring_turn(plans, moves, handed):
        later = []
        for (array, slab, axis, inner), (upward, downward) in zip(plans, moves):
            forth, forth_device = place.near(axis, 1)
            back, back_device = place.near(axis, -1)
            one, two = halves(inner, array)
            upward.wait_recv()
            held = slab(array, back, one)
            pair = [links.send(held, held, forth_device)]
            downward.wait_recv()
            held = slab(array, forth, two)
            pair.append(links.send(held, held, back_device))
            later.append(pair)
        for array, slab, axis, inner in plans:
            hand_over(slab(array, place.near(axis, -1)[0], ALL), handed)
            hand_over(slab(array, place.near(axis, 1)[0], ALL), handed)
        return later

    def ring_close(plans, later, handed):
        for (array, slab, axis, inner), pair in zip(plans, later):
            far, _ = place.near(axis, 2)
            for move, half in zip(pair, halves(inner, array)):
                move.wait_recv()
                hand_over(slab(array, far, half), handed)

    handed = [[] for _ in stages]
    ring, second = {}, {}

    def begin_inner(spot):
        ring[spot] = ring_start(stages[spot][0])

    def turn_inner(spot):
        ring[spot] = ring_turn(stages[spot][0], ring[spot], handed[spot])
        for array, slab, axis, inner in stages[spot][0]:
            hand_over(slab(array, getattr(place, axis), ALL), handed[spot])

    def end_inner(spot):
        ring_close(stages[spot][0], ring[spot], handed[spot])

    begin_inner(0)
    begin_inner(1)
    for move in gain_moves:
        move.wait_recv()
    gain_moves = [
        links.send(all_gains.at[z], all_gains.at[z], place.near("z", step)[1]) for step in (1, 2, 3)
    ]
    def begin_stage(spot):
        second[spot] = ring_start(stages[spot][1])

    def turn_stage(spot):
        second[spot] = ring_turn(stages[spot][1], second[spot], handed[spot])

    def end_stage(spot):
        ring_close(stages[spot][1], second[spot], handed[spot])
        for move in handed[spot]:
            move.wait_recv()

    turn_inner(0)
    turn_inner(1)
    end_inner(0)
    begin_stage(0)
    end_inner(1)
    begin_stage(1)
    for move in gain_moves:
        move.wait_recv()

    flat = lax.broadcasted_iota(jnp.int32, (128, 2176), 1)
    owner = lax.broadcasted_iota(jnp.int32, (128, 2176), 0)
    holds = (flat >= 17 * owner) & (flat < 17 * owner + 17)
    spread = over_rows(
        all_gains[...].reshape(128, 128).astype(low), jnp.where(holds, 1.0, 0.0).astype(low)
    )
    offset = jnp.sum(jnp.where(holds, flat - 17 * owner, 0), axis=0, keepdims=True)
    ordered = jnp.sum(jnp.where(owner == offset, spread, 0.0), axis=0, keepdims=True)
    gain_attn[...] = ordered[:, 0:D]
    gain_ffn[...] = ordered[:, D : 2 * D]
    heads = ordered[:, 2 * D : 2 * D + 128]
    turned_heads = pltpu.roll(heads, HD, 1)
    left = lax.broadcasted_iota(jnp.int32, (1, 128), 1) < HD
    gain_query[...] = jnp.where(left, heads, turned_heads)
    gain_key[...] = jnp.where(left, turned_heads, heads)

    @pl.loop(0, 8)
    def _(turn):
        rows = pl.ds(pl.multiple_of(turn * 32, 32), 32)
        block = tokens[rows, :].astype(wide)
        inverse = lax.rsqrt(jnp.mean(block * block, axis=1, keepdims=True) + EPS)
        norm[rows, :] = (block * inverse * gain_attn[...]).astype(low)

    def flip_into(source, target):
        @pl.loop(0, 8)
        def _(turn):
            cols = pl.ds(pl.multiple_of(turn * 128, 128), 128)
            target[cols, :] = source[:, cols].T

    def share(source, pair):
        keep(source, pair.at[0])
        pair_moves.append(links.send(source, pair.at[1], place.sibling))

    flip_into(norm, norm_t)
    share(norm_t, norm_pair)
    turn_stage(0)
    for spot in (2, 3, 4):
        begin_inner(spot)
    end_stage(0)
    keep(full_att, kept_att)
    keep(full_out, kept_out)

    @pl.loop(0, 4)
    def _(turn):
        cols = pl.ds(pl.multiple_of(turn * 512, 512), 512)
        raw[:, cols] = plain(norm[...], full_att[:, :, :, :, cols].reshape(D, 512))

    attention_heads(raw, cosine, signed_sine, segments, gain_query, gain_key, query, key, value, attended)
    for source, target in ((raw, raw_out), (query, query_out), (key, key_out), (value, value_out)):
        keep(source, target)
    turn_stage(1)
    for spot in (2, 3, 4):
        turn_inner(spot)

    @pl.loop(0, 2)
    def _(turn):
        cols = pl.ds(pl.multiple_of(turn * 512, 512), 512)
        block = plain(attended[...], full_out[:, :, :, :, cols].reshape(D, 512))
        middle[:, cols] = tokens[:, cols].astype(wide) + block

    @pl.loop(0, 8)
    def _(turn):
        rows = pl.ds(pl.multiple_of(turn * 32, 32), 32)
        block = middle[rows, :]
        middle_sum[rows, :] = block
        inverse = lax.rsqrt(jnp.mean(block * block, axis=1, keepdims=True) + EPS)
        mid[rows, :] = (block * inverse * gain_ffn[...]).astype(low)

    flip_into(attended, attended_t)
    share(attended_t, attended_pair)
    flip_into(mid, mid_t)
    share(mid_t, mid_pair)
    grad_mid[...] = jnp.zeros_like(grad_mid)

    used = {}

    def feed_forward(turn, between):
        slot = turn % 2
        if turn >= 2:
            for copy in used[turn - 2][:2]:
                copy.wait()
                own_copies.append(copy)
            for copy in used[turn - 2][2:]:
                copy.wait_send()
                links.gone.append(copy)
        cols = pl.ds(1152 * turn, 1152)

        def joint_cols(part):
            return full_joint[:, :, :, :, part * FF + 1152 * turn : part * FF + 1152 * turn + 1152].reshape(
                D, 1152
            )

        gate[...] = plain(mid[...], joint_cols(0))
        up[...] = plain(mid[...], joint_cols(1))
        grad_hidden[...] = near_rows(cotangent[...], full_down[turn].reshape(1152, D))

        @pl.loop(0, 16)
        def _(piece):
            rows = pl.ds(pl.multiple_of(piece * 16, 16), 16)
            gate_rows, up_rows, grad_rows = gate[rows, :], up[rows, :], grad_hidden[rows, :]
            sigmoid = 1.0 / (1.0 + jnp.exp(-gate_rows))
            swish = gate_rows * sigmoid
            hidden[rows, :] = (swish * up_rows).astype(low)
            slope = sigmoid * (1.0 + gate_rows * (1.0 - sigmoid))
            grad_joint[slot, 0, rows, :] = (grad_rows * up_rows * slope).astype(low)
            grad_joint[slot, 1, rows, :] = (grad_rows * swish).astype(low)

        for begin in range(0, 1152, 128):
            hidden_t[slot, begin : begin + 128, :] = hidden[:, begin : begin + 128].T
        used[turn] = [
            keep(hidden_t.at[slot], hidden_pair.at[0, cols]),
            keep(grad_joint.at[slot, core], joint_pair.at[0, :, cols]),
            links.send(hidden_t.at[slot], hidden_pair.at[1, cols], place.sibling),
            links.send(grad_joint.at[slot, other], joint_pair.at[1, :, cols], place.sibling),
        ]
        pair_moves.extend(used[turn][2:])
        if between is not None:
            between()
        middle_sum[...] += plain(hidden[...], full_down[turn].reshape(1152, D))
        for part in range(2):
            grad_mid[...] += near_rows(grad_joint[slot, part], joint_cols(part))

    def open_four():
        turn_stage(2)
        end_inner(4)
        begin_stage(4)

    for spot in (2, 3):
        end_inner(spot)
        begin_stage(spot)
    end_stage(1)
    feed_forward(0, open_four)
    end_stage(2)
    feed_forward(1, lambda: turn_stage(3))
    end_stage(3)
    feed_forward(2, lambda: turn_stage(4))
    end_stage(4)
    feed_forward(3, None)
    ffn_gains[...] = jnp.zeros_like(ffn_gains)

    @pl.loop(0, 8)
    def _(turn):
        rows = pl.ds(pl.multiple_of(turn * 32, 32), 32)
        block = middle[rows, :]
        inverse = lax.rsqrt(jnp.mean(block * block, axis=1, keepdims=True) + EPS)
        hat = block * inverse
        grad = grad_mid[rows, :]
        ffn_gains[...] += jnp.sum(grad * hat, axis=0, keepdims=True)
        grad = grad * gain_ffn[...]
        inner = jnp.mean(grad * hat, axis=1, keepdims=True)
        grad_middle[rows, :] = inverse * (grad - hat * inner) + cotangent[rows, :].astype(wide)
        result[rows, :] = middle_sum[rows, :].astype(low)

    for move in pair_moves:
        move.wait_recv()
    for copy in locals_:
        if not any((copy is done for done in own_copies)):
            copy.wait()
    links.finish()


def gather_all(att, out, joint, down, gains, tokens, cotangent, cosine, signed_sine, segments):
    any_space = pl.BlockSpec(memory_space=pl.ANY)
    vmem = pl.BlockSpec(memory_space=pltpu.VMEM)
    low, wide = jnp.bfloat16, jnp.float32
    outputs = [
        ((4, 4, 4, 16, 2 * HALF_ATT), low, any_space),
        ((4, 4, 4, 16, 2 * HALF_OUT), low, any_space),
        ((2, FF, 256), low, any_space),
        ((2, 256, FF), low, any_space),
        ((2, D, 256), low, any_space),
        ((2, D, 256), low, any_space),
        ((2, D, 256), low, any_space),
        ((2, 256, 512), low, any_space),
        ((256, 2048), wide, any_space),
        ((256, 1024), low, any_space),
        ((256, 512), low, any_space),
        ((256, 512), low, any_space),
        ((256, D), low, vmem),
        ((256, D), wide, vmem),
        ((1, D), wide, vmem),
        ((1, D), wide, vmem),
        ((1, 128), wide, vmem),
        ((1, 128), wide, vmem),
    ]
    scratch = [
        ((256, 2048), wide),
        ((256, 1024), low),
        ((256, 512), low),
        ((256, 512), low),
        ((4, 4, 4, 16, 2 * HALF_ATT), low),
        ((4, 4, 4, 16, 2 * HALF_OUT), low),
        ((4, 4, 4, 16, 2 * HALF_JOINT), low),
        ((4, 4, 18, 16, 2 * HALF_DOWN), low),
        ((8, HALF_ATT), wide),
        ((8, HALF_OUT), wide),
        ((8, HALF_JOINT), wide),
        ((16, HALF_ATT), low),
        ((16, HALF_OUT), low),
        ((16, HALF_JOINT), low),
        ((48, 2 * HALF_DOWN), wide),
        ((2, 48, HALF_DOWN), low),
        ((8, 48, HALF_DOWN), low),
        ((288, HALF_DOWN), wide),
        ((18, 16, HALF_DOWN), low),
        ((2, 8, 128), wide),
        ((4, 8, 128), wide),
        ((4, 4, 8, 128), wide),
        ((1, D), wide),
        ((1, 128), wide),
        ((256, D), low),
        ((256, D), low),
        ((256, D), low),
        ((D, 256), low),
        ((D, 256), low),
        ((D, 256), low),
        ((256, D), wide),
        ((256, D), wide),
        ((256, D), wide),
        ((256, 1152), wide),
        ((256, 1152), wide),
        ((256, 1152), wide),
        ((256, 1152), low),
        ((2, 1152, 256), low),
        ((2, 2, 256, 1152), low),
    ]
    operands = (att, out, joint, down, gains, tokens, cotangent, cosine, signed_sine, segments)
    return pl.pallas_call(
        gather_kernel,
        out_shape=tuple((jax.ShapeDtypeStruct(shape, kind) for shape, kind, _ in outputs)),
        in_specs=[vmem] * len(operands),
        out_specs=tuple((spec for _, _, spec in outputs)),
        scratch_shapes=[pltpu.VMEM(shape, kind) for shape, kind in scratch]
        + [
            pltpu.SemaphoreType.DMA((GATHER_COPIES,)),
            pltpu.SemaphoreType.DMA((GATHER_COPIES,)),
            pltpu.SemaphoreType.DMA((32,)),
        ],
        compiler_params=pltpu.CompilerParams(
            collective_id=0, has_side_effects=True, vmem_limit_bytes=60 * 1024 * 1024
        ),
        name="gather_weights",
    )(*operands)


class Product:
    def __init__(self, left, right, low, width, axis, buffers):
        self.left, self.right, self.low, self.width, self.axis = left, right, low, width, axis
        (
            self.far, self.side, self.p, self.m, self.pp, self.mm,
            self.p2, self.m2, self.pp2, self.mm2, self.third,
        ) = buffers
        self.inner = self.p.shape[1]
        self.chunk = min(width, 1152)

    def rows(self, token, spot, half):
        two = pl.ds(2 * half, 2)
        if self.axis == "z":
            block = self.left[token, spot, two]
        elif self.axis == "y":
            block = self.left[token, two, spot]
        else:
            block = self.left[token, two, :, spot]
        return block.reshape(2 * self.inner * 16, 256)

    def fill(self, spot, half, sink):
        first, second = self.rows(0, spot, half), self.rows(1, spot, half)

        def step(begin):
            source = pl.ds(pl.multiple_of(self.low + begin, 128), self.chunk)
            value = plain(first, self.right[0, :, source]) + plain(second, self.right[1, :, source])
            sink(
                pl.ds(pl.multiple_of(begin, 128), self.chunk),
                value.reshape(2, self.inner, 16, self.chunk),
            )

        if self.width == self.chunk:
            step(0)
        else:
            @pl.loop(0, self.width // self.chunk)
            def _(turn):
                step(turn * self.chunk)


def scatter_kernel(
    grad_middle, gain_attn, gain_query, gain_key, ffn_gains, *rest,
):
    sources, rest = rest[:FETCHED], rest[FETCHED:]
    grad_att, grad_out, grad_joint, grad_down, grad_gains, grad_squares, rows_out = rest[:7]
    scratch = list(rest[7:])

    def take(count):
        taken = scratch[:count]
        del scratch[:count]
        return taken

    buffers = [take(11) for _ in range(9)]
    chip_joint, chip_att, chip_out = take(3)
    rows_down, cut_down, got_down = take(3)
    gain_slots, square_slots = take(4), take(3)
    pad_down, own_gains, head_gains, grad_attended, grad_mixed = take(5)
    mixed_pair, mixed_away, branch_pair, branch_away = take(4)
    grad_rows, grad_key = take(2)
    fetched = take(FETCHED)
    send_sems, recv_sems, own_sems = take(3)
    fetches = [
        pltpu.make_async_copy(source, target, own_sems.at[spot])
        for spot, (source, target) in enumerate(zip(sources, fetched))
    ]
    for fetch in fetches:
        fetch.start()
    (
        mid_t, grad_joint_in, hidden_t, down_in, attended_t, weight_out, raw, query, key, value,
        cosine, signed_sine, segments, norm_t, weight_att, tokens,
    ) = fetched
    place = Place()
    core, z, y, x = place.core, place.z, place.y, place.x
    other = 1 - core
    links = Links(send_sems, recv_sems)
    place.greet()
    wide, low = jnp.float32, jnp.bfloat16
    one, two = pl.ds(0, 2), pl.ds(2, 2)

    def swap(buffer, value):
        buffer[core] = value
        return [links.send(buffer.at[core], buffer.at[core], place.sibling)]

    def deal(buffer, axis, value):
        spot = getattr(place, axis)
        buffer[spot] = value
        return [
            links.send(buffer.at[spot], buffer.at[spot], place.near(axis, step)[1])
            for step in (1, 2, 3)
        ]

    def total(moves, buffer, count):
        for move in moves:
            move.wait_recv()
        value = buffer[0]
        for spot in range(1, count):
            value = value + buffer[spot]
        return value

    def start_far(job):
        far, _ = place.near(job.axis, 2)
        forth, back = place.near(job.axis, 1)[1], place.near(job.axis, -1)[1]
        moves = []
        for half, device, target in ((0, forth, job.p), (1, back, job.m)):
            span = pl.ds(2 * half, 2)

            def sink(cols, block):
                job.far[span, :, :, cols] = block.astype(low)

            job.fill(far, half, sink)
            moves.append(links.send(job.far.at[span], target, device))
        return moves

    def start_sides(job):
        forth, forth_device = place.near(job.axis, 1)
        back, back_device = place.near(job.axis, -1)

        def sink_forth(cols, block):
            job.side[two, :, :, cols] = block.astype(low)

        def sink_back(cols, block):
            job.side[one, :, :, cols] = block.astype(low)

        job.fill(forth, 1, sink_forth)
        moves = [links.send(job.side.at[two], job.pp.at[two], forth_device)]
        job.fill(back, 0, sink_back)
        moves.append(links.send(job.side.at[one], job.mm.at[one], back_device))
        return moves

    def turn_first(job, early):
        forth, forth_device = place.near(job.axis, 1)
        back, back_device = place.near(job.axis, -1)

        def sink_forth(cols, block):
            job.p[:, :, :, cols] = (job.p[:, :, :, cols].astype(wide) + block).astype(low)

        def sink_back(cols, block):
            job.m[:, :, :, cols] = (job.m[:, :, :, cols].astype(wide) + block).astype(low)

        early[0].wait_recv()
        job.fill(forth, 0, sink_forth)
        moves = [links.send(job.p, job.pp.at[one], forth_device)]
        early[1].wait_recv()
        job.fill(back, 1, sink_back)
        moves.append(links.send(job.m, job.mm.at[two], back_device))
        return moves

    def close_first(job, moves):
        for move in moves:
            move.wait_recv()
        spot = getattr(place, job.axis)
        for half in range(2):
            span = pl.ds(2 * half, 2)

            def sink(cols, block):
                got = job.pp[span, :, :, cols].astype(wide) + job.mm[span, :, :, cols].astype(wide)
                job.pp[span, :, :, cols] = (got + block).astype(low)

            job.fill(spot, half, sink)

    def start_second(job, axis):
        half = job.inner // 2
        first, last = pl.ds(0, half), pl.ds(half, half)
        forth, forth_device = place.near(axis, 1)
        back, back_device = place.near(axis, -1)
        far, _ = place.near(axis, 2)
        early = [
            links.send(job.pp.at[far, first], job.p2, forth_device),
            links.send(job.pp.at[far, last], job.m2, back_device),
        ]
        later = [
            links.send(job.pp.at[forth, last], job.pp2.at[last], forth_device),
            links.send(job.pp.at[back, first], job.mm2.at[first], back_device),
        ]
        return early, later

    def turn_second(job, axis, early):
        half = job.inner // 2
        first, last = pl.ds(0, half), pl.ds(half, half)
        forth, forth_device = place.near(axis, 1)
        back, back_device = place.near(axis, -1)
        early[0].wait_recv()

        @pl.loop(0, half)
        def _(i):
            job.p2[i] = (job.p2[i].astype(wide) + job.pp[forth, i].astype(wide)).astype(low)

        moves = [links.send(job.p2, job.pp2.at[first], forth_device)]
        early[1].wait_recv()

        @pl.loop(0, half)
        def _(i):
            job.m2[i] = (job.m2[i].astype(wide) + job.pp[back, i + half].astype(wide)).astype(low)

        moves.append(links.send(job.m2, job.mm2.at[last], back_device))
        return moves

    def close_second(job, axis, moves):
        for move in moves:
            move.wait_recv()
        spot = getattr(place, axis)

        @pl.loop(0, job.inner)
        def _(i):
            value = job.pp[spot, i].astype(wide) + job.pp2[i].astype(wide) + job.mm2[i].astype(wide)
            job.pp2[i] = value.astype(low)

    def hand_out(job, axis):
        return [
            links.send(
                job.pp2.at[place.near(axis, step)[0]], job.third.at[step - 1], place.near(axis, step)[1]
            )
            for step in (1, 2, 3)
        ]

    swaps = []

    def finish_chip(job, axis, moves, chip, whole, half, squares):
        for move in moves:
            move.wait_recv()
        value = job.pp2[getattr(place, axis)].astype(wide)
        for step in range(3):
            value = value + job.third[step].astype(wide)
        chip[:, job.low : job.low + job.width] = value
        cols = lanes(core, half, job.low, job.width)
        swaps.append(
            links.send(
                chip.at[pl.ds(pl.multiple_of(8 * other, 8), 8), pl.ds(job.low, job.width)],
                whole.at[:, cols],
                place.sibling,
            )
        )
        whole[:, cols] = chip[
            pl.ds(pl.multiple_of(8 * core, 8), 8), job.low : job.low + job.width
        ]
        for begin in range(job.low, job.low + job.width, 128):
            for row in (0, 8):
                piece = chip[row : row + 8, begin : begin + 128]
                squares = squares + piece * piece
        return squares

    joint_a = Product(mid_t, grad_joint_in, 0, CUT, "z", buffers[0])
    joint_b = Product(mid_t, grad_joint_in, CUT, CUT, "y", buffers[1])
    joint_c = Product(mid_t, grad_joint_in, 2 * CUT, CUT, "x", buffers[2])
    joint_d = Product(mid_t, grad_joint_in, 3 * CUT, CUT, "x", buffers[3])
    down_a = Product(hidden_t, down_in, 0, 256, "z", buffers[4])
    down_b = Product(hidden_t, down_in, 256, 256, "y", buffers[5])
    att_a = Product(norm_t, mixed_pair, 0, 512, "z", buffers[6])
    att_b = Product(norm_t, mixed_pair, 512, 512, "y", buffers[7])
    out_c = Product(attended_t, branch_pair, 0, 512, "x", buffers[8])
    wave_one = [joint_a, joint_b, joint_c]
    wave_two = [joint_d, down_a, down_b]
    wave_three = [out_c, att_a, att_b]
    second_axis = {
        id(job): {"z": "y", "y": "z", "x": "z"}[job.axis] for job in wave_one + wave_two + wave_three
    }
    third_axis = {
        id(job): "y" if job.axis == "x" else "x" for job in wave_one + wave_two + wave_three
    }

    for begin in range(0, 1024, 256):
        branch_away[:, begin : begin + 256] = grad_middle[:, begin : begin + 256].astype(low)
    branch_pair[0] = branch_away[:, lanes(core, 512, 0, 512)]
    branch_move = links.send(
        branch_away.at[:, lanes(other, 512, 0, 512)], branch_pair.at[1], place.sibling
    )
    early, moves, later, last = {}, {}, {}, {}

    def send_far(jobs):
        for job in jobs:
            early[id(job)] = start_far(job)

    def send_sides(jobs):
        for job in jobs:
            moves[id(job)] = start_sides(job)

    def turn(jobs):
        for job in jobs:
            moves[id(job)] += turn_first(job, early[id(job)])

    def close(jobs):
        for job in jobs:
            close_first(job, moves[id(job)])
            early[id(job)], later[id(job)] = start_second(job, second_axis[id(job)])

    def turn_again(jobs):
        for job in jobs:
            later[id(job)] += turn_second(job, second_axis[id(job)], early[id(job)])

    def close_again(jobs):
        for job in jobs:
            close_second(job, second_axis[id(job)], later[id(job)])
            if job.inner == 4:
                last[id(job)] = hand_out(job, third_axis[id(job)])

    fetches[0].wait()
    fetches[1].wait()
    send_far(wave_one)
    send_sides(wave_one)
    for fetch in fetches[2:]:
        fetch.wait()

    @pl.loop(0, 4)
    def _(spot):
        cols = pl.ds(pl.multiple_of(spot * 256, 256), 256)
        grad_attended[:, cols] = near_rows(branch_away[...], weight_out[cols, :]).astype(low)

    turn(wave_one)
    send_far(wave_two)

    attention_heads_back(
        grad_attended, raw, query, key, value, cosine, signed_sine, segments, gain_query, gain_key,
        mixed_away, head_gains, grad_rows, grad_key,
    )
    mixed_pair[0] = mixed_away[:, lanes(core, 1024, 0, 1024)]
    mixed_move = links.send(
        mixed_away.at[:, lanes(other, 1024, 0, 1024)], mixed_pair.at[1], place.sibling
    )
    send_sides(wave_two)
    close(wave_one)
    branch_move.wait_recv()
    mixed_move.wait_recv()
    send_far(wave_three)
    send_sides(wave_three)
    turn(wave_two)
    turn_again(wave_one)

    @pl.loop(0, 4)
    def _(turn):
        cols = pl.ds(pl.multiple_of(turn * 256, 256), 256)
        grad_rows[:, cols] = near_rows(mixed_away[...], weight_att[cols, :])

    own_gains[...] = jnp.zeros_like(own_gains)

    @pl.loop(0, 8)
    def _(turn):
        rows = pl.ds(pl.multiple_of(turn * 32, 32), 32)
        block = tokens[rows, :].astype(wide)
        inverse = lax.rsqrt(jnp.mean(block * block, axis=1, keepdims=True) + EPS)
        hat = block * inverse
        grad = grad_rows[rows, :]
        own_gains[0:1, :] += jnp.sum(grad * hat, axis=0, keepdims=True)
        grad = grad * gain_attn[...]
        inner = jnp.mean(grad * hat, axis=1, keepdims=True)
        grad_rows[rows, :] = inverse * (grad - hat * inner) + grad_middle[rows, :]

    rows_copy = pltpu.make_async_copy(grad_rows, rows_out, own_sems.at[FETCHED])
    rows_copy.start()
    own_gains[1:2, :] = ffn_gains[...]
    own_gains[2:4, 0:128] = head_gains[...]
    gain_moves = swap(gain_slots[0], own_gains[...])
    close(wave_two)
    gain_moves = deal(gain_slots[1], "x", total(gain_moves, gain_slots[0], 2))
    turn(wave_three)
    close_again(wave_one)
    turn_again(wave_two)
    gain_moves = deal(gain_slots[2], "y", total(gain_moves, gain_slots[1], 4))
    close(wave_three)
    close_again(wave_two)
    rows_down[288:296, :] = jnp.zeros((8, 512), wide)
    rows_down[0:288, 0:256] = down_a.pp2[...].astype(wide).reshape(288, 256)
    rows_down[0:288, 256:512] = down_b.pp2[...].astype(wide).reshape(288, 256)
    for spot in range(8):
        cut_down[spot] = rows_down[spot * DOWN_ROWS : spot * DOWN_ROWS + 40, :]
    down_moves = []
    for step in range(4):
        to = lax.rem(x + step, 4)
        for flip in range(2):
            to_core = lax.rem(core + flip, 2)
            if step or flip:
                down_moves.append(
                    links.send(
                        cut_down.at[2 * to + to_core],
                        got_down.at[2 * step + flip],
                        place.at(x=to, core=to_core),
                    )
                )
    got_down[0] = cut_down[2 * x + core]
    squares = jnp.zeros((8, 128), wide)
    for job in wave_one:
        squares = finish_chip(
            job, third_axis[id(job)], last[id(job)], chip_joint, grad_joint, HALF_JOINT, squares
        )
    gain_moves = deal(gain_slots[3], "z", total(gain_moves, gain_slots[2], 4))
    turn_again(wave_three)
    squares = finish_chip(
        joint_d, third_axis[id(joint_d)], last[id(joint_d)], chip_joint, grad_joint, HALF_JOINT, squares
    )
    close_again(wave_three)
    for move in down_moves:
        move.wait_recv()
    live = lax.broadcasted_iota(jnp.int32, (40, 512), 0) < DOWN_ROWS
    for flip in range(2):
        value_down = got_down[flip]
        for step in range(1, 4):
            value_down = value_down + got_down[2 * step + flip]
        half_core = lax.rem(core + flip, 2)
        pad_down[:, lanes(half_core, 512, 0, 512)] = jnp.where(live, value_down, 0.0)
    grad_down[...] = pad_down[0:DOWN_ROWS, :]
    for row in range(0, 40, 8):
        for col in range(0, 1024, 128):
            piece = pad_down[row : row + 8, col : col + 128]
            squares = squares + piece * piece
    gain_sums = total(gain_moves, gain_slots[3], 4)
    heads = gain_sums[2:4, 0:128]
    heads = heads + pltpu.roll(heads, HD, 1)
    left = lax.broadcasted_iota(jnp.int32, (1, 128), 1) < HD
    heads = jnp.where(left, heads[0:1], heads[1:2])
    me = place.at()
    picked = jnp.zeros((1, 128), wide)
    for begin, size, part in (
        (0, D, gain_sums[0:1]), (D, D, gain_sums[1:2]), (2 * D, 128, heads)
    ):
        entry = lax.broadcasted_iota(jnp.int32, (size, 128), 0) + begin
        wanted = lax.broadcasted_iota(jnp.int32, (size, 128), 1) + 17 * me
        picked = picked + lax.dot_general(
            part, jnp.where(entry == wanted, 1.0, 0.0), (((1,), (0,)), ((), ())),
            precision=lax.Precision.HIGHEST, preferred_element_type=wide,
        )
    grad_gains[...] = picked
    gain_squares = heads * heads
    for col in range(0, D, 128):
        for part in range(2):
            piece = gain_sums[part : part + 1, col : col + 128]
            gain_squares = gain_squares + piece * piece
    once = (lax.broadcasted_iota(jnp.int32, (8, 128), 0) == 0) & (me == 0)
    squares = squares + jnp.where(once, gain_squares, 0.0)
    for job, chip, whole, half in (
        (out_c, chip_out, grad_out, HALF_OUT),
        (att_a, chip_att, grad_att, HALF_ATT),
        (att_b, chip_att, grad_att, HALF_ATT),
    ):
        squares = finish_chip(job, third_axis[id(job)], last[id(job)], chip, whole, half, squares)
    seat = 2 * x + core
    square_slots[0][seat] = squares
    square_moves = []
    for step in range(4):
        to = lax.rem(x + step, 4)
        for flip in range(2):
            if step or flip:
                square_moves.append(
                    links.send(
                        square_slots[0].at[seat],
                        square_slots[0].at[seat],
                        place.at(x=to, core=lax.rem(core + flip, 2)),
                    )
                )
    square_moves = deal(square_slots[1], "y", total(square_moves, square_slots[0], 8))
    square_moves = deal(square_slots[2], "z", total(square_moves, square_slots[1], 4))
    grad_squares[...] = total(square_moves, square_slots[2], 4)
    for move in swaps:
        move.wait_recv()
    rows_copy.wait()
    links.finish()


def scatter_all(*operands):
    vmem = pl.BlockSpec(memory_space=pltpu.VMEM)
    any_space = pl.BlockSpec(memory_space=pl.ANY)
    sources = operands[len(operands) - FETCHED :]
    low, wide = jnp.bfloat16, jnp.float32

    def ring_buffers(inner, width):
        tail = (16, width)
        half, whole = (2, inner) + tail, (4, inner) + tail
        shapes = (whole, whole, half, half, whole, whole)
        shapes += ((inner // 2,) + tail, (inner // 2,) + tail, (inner,) + tail, (inner,) + tail)
        shapes += ((3,) + tail,)
        return [pltpu.VMEM(shape, low) for shape in shapes]

    scratch = []
    for inner, width in ((4, CUT),) * 4 + ((18, 256),) * 2 + ((4, 512),) * 3:
        scratch += ring_buffers(inner, width)
    scratch += [pltpu.VMEM((16, width), wide) for width in (HALF_JOINT, HALF_ATT, HALF_OUT)]
    scratch += [
        pltpu.VMEM((296, 512), wide),
        pltpu.VMEM((8, 40, 512), wide),
        pltpu.VMEM((8, 40, 512), wide),
    ]
    scratch += [pltpu.VMEM((count, 8, 1024), wide) for count in (2, 4, 4, 4)]
    scratch += [pltpu.VMEM((count, 8, 128), wide) for count in (8, 4, 4)]
    scratch += [
        pltpu.VMEM((40, 1024), wide),
        pltpu.VMEM((8, 1024), wide),
        pltpu.VMEM((2, 128), wide),
        pltpu.VMEM((256, 1024), low),
        pltpu.VMEM((8, 128), low),
        pltpu.VMEM((2, 256, 1024), low),
        pltpu.VMEM((256, 2048), low),
        pltpu.VMEM((2, 256, 512), low),
        pltpu.VMEM((256, 1024), low),
        pltpu.VMEM((256, 1024), wide),
        pltpu.VMEM((256, 512), wide),
    ]
    scratch += [pltpu.VMEM(source.shape, source.dtype) for source in sources]
    scratch += [
        pltpu.SemaphoreType.DMA((SCATTER_COPIES,)),
        pltpu.SemaphoreType.DMA((SCATTER_COPIES,)),
        pltpu.SemaphoreType.DMA((FETCHED + 1,)),
    ]
    return pl.pallas_call(
        scatter_kernel,
        out_shape=(
            jax.ShapeDtypeStruct((8, 2 * HALF_ATT), wide),
            jax.ShapeDtypeStruct((8, 2 * HALF_OUT), wide),
            jax.ShapeDtypeStruct((8, 2 * HALF_JOINT), wide),
            jax.ShapeDtypeStruct((DOWN_ROWS, D), wide),
            jax.ShapeDtypeStruct((1, 128), wide),
            jax.ShapeDtypeStruct((8, 128), wide),
            jax.ShapeDtypeStruct((256, D), wide),
        ),
        in_specs=[vmem] * (len(operands) - FETCHED) + [any_space] * FETCHED,
        out_specs=(vmem,) * 6 + (any_space,),
        scratch_shapes=scratch,
        compiler_params=pltpu.CompilerParams(
            collective_id=1, has_side_effects=True, vmem_limit_bytes=60 * 1024 * 1024
        ),
        name="scatter_gradients",
    )(*operands)


def update_kernel(clip_limit, rates, decays, *refs):
    count = len(rates)
    squares, refs = refs[0], refs[1:]
    operands, refs = refs[: 4 * count], refs[4 * count :]
    moved, refs = refs[:2], refs[2:]
    norm_out, outs, refs = refs[0], refs[1 : 3 * count + 1], refs[3 * count + 1 :]
    targets, held, sems = refs[:2], refs[2:-1], refs[-1]
    copies = [
        pltpu.make_async_copy(source, target, sems.at[spot])
        for spot, (source, target) in enumerate(zip(operands + moved, held + targets))
    ]
    for copy in copies:
        copy.start()
    grads, weights, firsts, seconds = (held[k * count : k * count + count] for k in range(4))
    norm = jnp.sqrt(jnp.sum(squares[...], keepdims=True))
    norm_out[...] = norm
    factor = clip_limit / jnp.maximum(norm, clip_limit)
    for spot in range(count):
        for part in range(4):
            copies[part * count + spot].wait()
        width = weights[spot].shape[1]
        step = min(width, 512)
        for begin in range(0, width, step):
            cols = slice(begin, begin + step)
            updated = adam_update(
                weights[spot][:, cols],
                firsts[spot][:, cols],
                seconds[spot][:, cols],
                grads[spot][:, cols] * factor,
                rates[spot],
                decays[spot],
            )
            for part in range(3):
                outs[part * count + spot][:, cols] = updated[part]
    for copy in copies[4 * count :]:
        copy.wait()


def update_all(clip_limit, rates, decays, squares, grads, weights, firsts, seconds, moved):
    vmem = pl.BlockSpec(memory_space=pltpu.VMEM)
    any_space = pl.BlockSpec(memory_space=pl.ANY)
    fetched = (*grads, *weights, *firsts, *seconds)
    operands = (squares, *fetched, *moved)
    shapes = [jax.ShapeDtypeStruct((1, 1), jnp.float32)]
    shapes += [jax.ShapeDtypeStruct(weight.shape, jnp.float32) for weight in weights] * 3
    shapes += [jax.ShapeDtypeStruct(array.shape, array.dtype) for array in moved]
    return pl.pallas_call(
        functools.partial(update_kernel, clip_limit, rates, decays),
        out_shape=tuple(shapes),
        in_specs=[vmem] + [any_space] * (len(fetched) + len(moved)),
        out_specs=(vmem,) * len(shapes),
        scratch_shapes=[pltpu.VMEM(array.shape, array.dtype) for array in fetched]
        + [pltpu.SemaphoreType.DMA((len(fetched) + len(moved),))],
        compiler_params=pltpu.CompilerParams(vmem_limit_bytes=60 * 1024 * 1024),
        name="update_weights",
    )(*operands)

def adam_update(weight, first, second, gradient, rate, decay):
    new_first = BETA_ONE * first + (1.0 - BETA_ONE) * gradient
    new_second = SQUARE_DAMPING * second + (1.0 - SQUARE_DAMPING) * gradient * gradient
    corrected = new_first / (1.0 - BETA_ONE**STEP)
    divisor = jnp.sqrt(new_second / (1.0 - SQUARE_DAMPING**STEP)) + MOMENT_FLOOR
    return (weight - rate * (corrected / divisor + decay * weight), new_first, new_second)


def per_device(
    inputs,
    cotangent,
    segments,
    positions,
    attention_weight,
    output_weight,
    joint_projection_matrix,
    down_weight,
    gains,
    first_attend,
    first_output,
    first_gate_up,
    first_down,
    first_gains,
    second_attend,
    second_output,
    second_gate_up,
    second_down,
    second_gains,
):
    params = (attention_weight, output_weight, joint_projection_matrix, down_weight, gains)
    devices = lax.axis_size("fsdp")
    tokens = inputs.shape[0] * inputs.shape[2]
    rows = inputs.reshape(tokens, D)
    lane = jnp.arange(2 * HD)
    exponent = -(lane % (HD // 2)).astype(jnp.float32) * 2.0 / HD
    phases = positions.reshape(tokens, 1).astype(jnp.float32) * THETA**exponent
    cosine = jnp.cos(phases)
    signed_sine = jnp.sin(phases) * jnp.where(lane % HD < HD // 2, -1.0, 1.0)
    segments = segments[:, 0]
    (
        low_att, low_out, hidden_pair, joint_pair, norm_pair, attended_pair, mid_pair, down_pair,
        raw, query, key, value, result, grad_middle, ffn_gains, gain_attn, gain_query, gain_key,
    ) = gather_all(
        *params[:4], gains.reshape(1, -1), rows, cotangent.reshape(tokens, D), cosine, signed_sine, segments
    )
    *reduced, square_sums, grad_rows = scatter_all(
        grad_middle,
        gain_attn,
        gain_query,
        gain_key,
        ffn_gains,
        mid_pair.reshape(2, 4, 4, 4, 16, tokens),
        joint_pair,
        hidden_pair.reshape(2, 4, 4, 18, 16, tokens),
        down_pair,
        attended_pair.reshape(2, 4, 4, 4, 16, tokens),
        low_out.reshape(D, 2 * HALF_OUT),
        raw,
        query,
        key,
        value,
        cosine,
        signed_sine,
        segments,
        norm_pair.reshape(2, 4, 4, 4, 16, tokens),
        low_att.reshape(D, 2 * HALF_ATT),
        rows,
    )
    token_count = inputs.shape[0] * inputs.shape[1] * inputs.shape[2] * devices
    param_count = sum((weight.size for weight in params)) * devices
    clip_limit = CLIP_COEF * math.sqrt(token_count * param_count)
    step_rates = (
        0.8 / math.sqrt(D),
        0.8 / math.sqrt(H * HD // 16),
        0.8 / math.sqrt(D),
        0.8 / math.sqrt(FF),
        GAIN_RATE,
    )
    decays = (DECAY, DECAY, DECAY, DECAY, 0.0)
    firsts = (first_attend, first_output, first_gate_up, first_down, first_gains)
    seconds = (second_attend, second_output, second_gate_up, second_down, second_gains)
    reduced[4] = reduced[4][:, : gains.shape[0]]

    def flat_rows(arrays):
        return arrays[:4] + (arrays[4].reshape(1, -1),)

    grad_norm, *updated, result, grad_rows = update_all(
        clip_limit, step_rates, decays, square_sums, reduced,
        flat_rows(params), flat_rows(firsts), flat_rows(seconds), (result, grad_rows),
    )
    grad_norm = grad_norm.reshape(())
    for slot in (4, 9, 14):
        updated[slot] = updated[slot].reshape(-1)
    result = result.reshape(inputs.shape)
    grad_inputs = grad_rows.reshape(inputs.shape)
    return (
        result,
        grad_inputs,
        grad_norm,
        *updated,
    )


def solution(mesh):
    in_specs = (
        P(None, "fsdp", None, None),
        P(None, "fsdp", None, None),
        P(None, "fsdp", None),
        P(None, "fsdp", None),
        P("fsdp", None),
        P("fsdp", None),
        P("fsdp", None),
        P("fsdp", None),
        P("fsdp"),
        P("fsdp", None),
        P("fsdp", None),
        P("fsdp", None),
        P("fsdp", None),
        P("fsdp"),
        P("fsdp", None),
        P("fsdp", None),
        P("fsdp", None),
        P("fsdp", None),
        P("fsdp"),
    )
    out_specs = (
        P(None, "fsdp", None, None),
        P(None, "fsdp", None, None),
        P(),
        P("fsdp", None),
        P("fsdp", None),
        P("fsdp", None),
        P("fsdp", None),
        P("fsdp"),
        P("fsdp", None),
        P("fsdp", None),
        P("fsdp", None),
        P("fsdp", None),
        P("fsdp"),
        P("fsdp", None),
        P("fsdp", None),
        P("fsdp", None),
        P("fsdp", None),
        P("fsdp"),
    )
    return jax.shard_map(
        per_device, mesh=mesh, in_specs=in_specs, out_specs=out_specs, check_vma=False
    )
```

```python
import functools
import math

import jax
import jax.numpy as jnp
from jax import lax
from jax.experimental import pallas as pl
from jax.experimental.pallas import tpu as pltpu
from jax.sharding import PartitionSpec as P

D = 1024
H = 16
KV = 8
HD = 64
FF = 4608
STEP = 10


EPS = 1e-05
THETA = 1000000.0
CLIP_COEF = 0.02
BETA_ONE = 0.9
SQUARE_DAMPING = 0.95
MOMENT_FLOOR = 1e-08
DECAY = 0.1
GAIN_RATE = 0.3
BLOCKED = -1e30
GATHER_COPIES = 336
SCATTER_COPIES = 176
FETCHED = 16


def counted(segments):
    wide = jnp.broadcast_to(segments.astype(jnp.float32), (128, 128))
    row = lax.broadcasted_iota(jnp.int32, (128, 128), 0)
    col = lax.broadcasted_iota(jnp.int32, (128, 128), 1)
    allowed = (wide == wide.T) & (col <= row)
    return jnp.concatenate([allowed, allowed], axis=0)


MESH = pl.DeviceIdType.MESH
HALF_ATT, HALF_OUT, HALF_JOINT, HALF_DOWN = 1024, 512, FF, 512
CUT = 1152
LAST = FF - 2 * CUT
DOWN_ROWS = FF // 128


class Place:
    def __init__(self):
        me = lax.axis_index("fsdp")
        self.core = lax.rem(me, 2)
        self.x = lax.rem(lax.div(me, 2), 4)
        self.y = lax.rem(lax.div(me, 8), 4)
        self.z = lax.div(me, 32)
        self.sibling = self.at(core=1 - self.core)

    def at(self, z=None, y=None, x=None, core=None):
        z = self.z if z is None else z
        y = self.y if y is None else y
        x = self.x if x is None else x
        core = self.core if core is None else core
        return ((z * 4 + y) * 4 + x) * 2 + core

    def near(self, axis, step):
        spot = lax.rem(getattr(self, axis) + step + 4, 4)
        return spot, self.at(**{axis: spot})

    def greet(self):
        barrier = pltpu.get_barrier_semaphore()
        others = [self.sibling]
        for step in (1, 2, 3):
            spot, device = self.near("x", step)
            others += [device, self.at(x=spot, core=1 - self.core)]
            others += [self.near("y", step)[1], self.near("z", step)[1]]
        for device in others:
            pl.semaphore_signal(barrier, inc=1, device_id=(device,), device_id_type=MESH)
        pl.semaphore_wait(barrier, len(others))


class Links:
    def __init__(self, send_sems, recv_sems):
        self.send_sems, self.recv_sems = send_sems, recv_sems
        self.copies, self.gone = [], []

    def send(self, source, target, device):
        slot = len(self.copies)
        copy = pltpu.make_async_remote_copy(
            src_ref=source,
            dst_ref=target,
            send_sem=self.send_sems.at[slot],
            recv_sem=self.recv_sems.at[slot],
            device_id=(device,),
            device_id_type=MESH,
        )
        copy.start()
        self.copies.append(copy)
        return copy

    def finish(self):
        assert len(self.copies) <= self.send_sems.shape[0]
        for copy in self.copies:
            if not any((copy is done for done in self.gone)):
                copy.wait_send()


def lanes(core, half, low, width):
    return pl.ds(pl.multiple_of(core * half + low, 128), width)


ALL = slice(None)


def near_rows(left, right):
    return lax.dot_general(left, right, (((1,), (1,)), ((), ())), preferred_element_type=jnp.float32)


def over_rows(left, right):
    return lax.dot_general(left, right, (((0,), (0,)), ((), ())), preferred_element_type=jnp.float32)


def plain(left, right):
    return lax.dot_general(left, right, (((1,), (0,)), ((), ())), preferred_element_type=jnp.float32)


def head_mean(values):
    row = lax.broadcasted_iota(jnp.int32, (128, 128), 0) < HD
    col = lax.broadcasted_iota(jnp.int32, (128, 128), 1) < HD
    same = jnp.where(row == col, 1.0, 0.0).astype(jnp.bfloat16)
    coarse = values.astype(jnp.bfloat16)
    fine = (values - coarse.astype(jnp.float32)).astype(jnp.bfloat16)
    sums = plain(coarse, same) + plain(fine, same)
    return sums * (1.0 / HD)


def partner(values):
    lane = lax.broadcasted_iota(jnp.int32, values.shape, 1)
    return jnp.where(
        lax.rem(lane, HD) < HD // 2, pltpu.roll(values, 128 - HD // 2, 1), pltpu.roll(values, HD // 2, 1)
    )


def left_lanes():
    return lax.broadcasted_iota(jnp.int32, (128, 128), 1) < HD


def both(block):
    block = block.astype(jnp.float32)
    turned = pltpu.roll(block, HD, 1)
    return (
        jnp.where(left_lanes(), block, turned).astype(jnp.bfloat16),
        jnp.where(left_lanes(), turned, block).astype(jnp.bfloat16),
    )


def stacked(block):
    block = block.astype(jnp.float32)
    return jnp.concatenate(
        [jnp.where(left_lanes(), block, 0.0), jnp.where(left_lanes(), 0.0, block)], axis=0
    ).astype(jnp.bfloat16)


def attention_heads(
    raw, cosine, signed_sine, segments, gain_query, gain_key, query, key, value, attended
):
    wide, low = jnp.float32, jnp.bfloat16
    turned = []
    for block in range(12):
        mixed = raw[:, block * 128 : block * 128 + 128]
        gain = gain_query if block < 8 else gain_key
        hat = mixed * lax.rsqrt(head_mean(mixed * mixed) + EPS) * gain[...]
        turned.append((hat * cosine[...] + partner(hat) * signed_sine[...]).astype(low))
        if block % 4 == 3:
            target, start = (query, block - 3) if block < 8 else (key, 0)
            for spot, piece in enumerate(turned):
                target[:, (start + spot) * 128 : (start + spot) * 128 + 128] = piece
            turned = []
    value[...] = raw[:, (H + KV) * HD :].astype(low)
    counts = []
    for sequence in range(2):
        counts.append(counted(segments[sequence : sequence + 1, :]))

    @pl.loop(0, 4)
    def _(pair):
        pair_cols = pl.ds(pl.multiple_of(pair * 128, 128), 128)
        cols = [pl.ds(pl.multiple_of(pair * 256 + parity * 128, 128), 128) for parity in range(2)]
        units = []
        for sequence in range(2):
            rows = slice(sequence * 128, sequence * 128 + 128)
            keys, values = both(key[rows, pair_cols]), both(value[rows, pair_cols])
            for parity in range(2):
                units.append(
                    (sequence, rows, cols[parity], stacked(query[rows, cols[parity]]), keys[parity], values[parity])
                )
        scores = [
            jnp.where(counts[unit[0]], near_rows(unit[3], unit[4]) * HD ** (-0.5), BLOCKED) for unit in units
        ]
        raised = [jnp.exp(score - jnp.max(score, axis=1, keepdims=True)) for score in scores]
        soft = [(rise / jnp.sum(rise, axis=1, keepdims=True)).astype(low) for rise in raised]
        parts = [plain(weights, unit[5]) for weights, unit in zip(soft, units)]
        for unit, part in zip(units, parts):
            attended[unit[1], unit[2]] = jnp.where(left_lanes(), part[0:128], part[128:256]).astype(low)


def attention_heads_back(
    grad_att, raw, query, key, value, cosine, signed_sine, segments, gain_query, gain_key,
    grad_mixed, head_gains, grad_query, grad_key,
):
    wide, low = jnp.float32, jnp.bfloat16
    counts = []
    for sequence in range(2):
        counts.append(counted(segments[sequence : sequence + 1, :]))

    @pl.loop(0, 4)
    def _(pair):
        pair_cols = pl.ds(pl.multiple_of(pair * 128, 128), 128)
        cols = [pl.ds(pl.multiple_of(pair * 256 + parity * 128, 128), 128) for parity in range(2)]
        units = []
        for sequence in range(2):
            rows = slice(sequence * 128, sequence * 128 + 128)
            keys, values = both(key[rows, pair_cols]), both(value[rows, pair_cols])
            for parity in range(2):
                units.append(
                    (
                        counts[sequence],
                        stacked(query[rows, cols[parity]]),
                        stacked(grad_att[rows, cols[parity]]),
                        keys[parity],
                        values[parity],
                    )
                )
        scores = [
            jnp.where(count, near_rows(queries, keys) * HD ** (-0.5), BLOCKED)
            for count, queries, _, keys, _ in units
        ]
        raised = [jnp.exp(score - jnp.max(score, axis=1, keepdims=True)) for score in scores]
        soft = [rise / jnp.sum(rise, axis=1, keepdims=True) for rise in raised]
        grad_soft = [near_rows(grads, values) for _, _, grads, _, values in units]
        grad_scores = [
            (weights * (grad - jnp.sum(grad * weights, axis=1, keepdims=True))).astype(low)
            for weights, grad in zip(soft, grad_soft)
        ]
        value_parts = [over_rows(weights.astype(low), unit[2]) for weights, unit in zip(soft, units)]
        key_parts = [over_rows(grad, unit[1]) * HD ** (-0.5) for grad, unit in zip(grad_scores, units)]
        query_parts = [plain(grad, unit[3]) * HD ** (-0.5) for grad, unit in zip(grad_scores, units)]
        value_parts = [part + pltpu.roll(part, HD, 1) for part in value_parts]
        key_parts = [part + pltpu.roll(part, HD, 1) for part in key_parts]
        value_cols = pl.ds(pl.multiple_of((H + KV) * HD + pair * 128, 128), 128)
        for sequence in range(2):
            rows = slice(sequence * 128, sequence * 128 + 128)
            even, odd = 2 * sequence, 2 * sequence + 1
            for spot, unit in enumerate((even, odd)):
                part = query_parts[unit]
                grad_query[rows, cols[spot]] = jnp.where(left_lanes(), part[0:128], part[128:256])
            grad_key[rows, pair_cols] = jnp.where(left_lanes(), key_parts[even], key_parts[odd])
            grad_mixed[rows, value_cols] = jnp.where(
                left_lanes(), value_parts[even], value_parts[odd]
            ).astype(low)

    gains = []
    for block in range(12):
        source, spot, gain = (grad_query, block, gain_query) if block < 8 else (grad_key, block - 8, gain_key)
        grad = source[:, spot * 128 : spot * 128 + 128]
        grad = grad * cosine[...] - partner(grad) * signed_sine[...]
        mixed = raw[:, block * 128 : block * 128 + 128]
        inverse = lax.rsqrt(head_mean(mixed * mixed) + EPS)
        hat = mixed * inverse
        gains.append(jnp.sum(grad * hat, axis=0, keepdims=True))
        grad = grad * gain[...]
        grad_mixed[:, block * 128 : block * 128 + 128] = (
            inverse * (grad - hat * head_mean(grad * hat))
        ).astype(low)
    head_gains[0:1, :] = sum(gains[1:8], gains[0])
    head_gains[1:2, :] = sum(gains[9:12], gains[8])


def gather_kernel(
    att, out, joint, down, gains, tokens, cotangent, cosine, signed_sine, segments,
    kept_att, kept_out, hidden_pair, joint_pair, norm_pair, attended_pair, mid_pair, down_pair,
    raw_out, query_out, key_out, value_out,
    result, grad_middle, ffn_gains, gain_attn, gain_query, gain_key,
    raw, query, key, value, full_att, full_out, full_joint, full_down,
    got_att, got_out, got_joint, low_att, low_out, low_joint,
    pad_down, send_down, got_down, rows_down, low_down,
    core_gains, x_gains, all_gains, gain_ffn, pad_gains,
    norm, attended, mid, norm_t, attended_t, mid_t, middle, middle_sum, grad_mid,
    gate, up, grad_hidden, hidden, hidden_t, grad_joint,
    send_sems, recv_sems, own_sems,
):
    place = Place()
    core, z, y, x = place.core, place.z, place.y, place.x
    wide, low = jnp.float32, jnp.bfloat16
    links = Links(send_sems, recv_sems)
    place.greet()
    other = 1 - core
    seat = 2 * x + core
    locals_ = []

    def keep(source, target):
        copy = pltpu.make_async_copy(source, target, own_sems.at[len(locals_)])
        copy.start()
        locals_.append(copy)
        return copy

    swaps = []
    for source, target, half in (
        (att, got_att, HALF_ATT), (out, got_out, HALF_OUT), (joint, got_joint, HALF_JOINT)
    ):
        swaps.append(links.send(source.at[:, lanes(other, half, 0, half)], target, place.sibling))
    row = lax.broadcasted_iota(jnp.int32, (8, 128), 0)
    pad_gains[...] = jnp.zeros_like(pad_gains)
    pad_gains[:, 0:17] = gains[...]
    core_gains[core] = jnp.where(row == seat, pad_gains[...], 0.0)
    gain_swap = links.send(core_gains.at[core], core_gains.at[core], place.sibling)
    own_copies = []

    def chip_block(copy, source, target, chip, full, half):
        copy.wait_recv()
        for begin in range(0, half, 512):
            own = source[:, lanes(core, half, begin, 512)]
            got = target[:, begin : begin + 512]
            first = jnp.where(core == 0, own, got)
            second = jnp.where(core == 0, got, own)
            chip[:, begin : begin + 512] = jnp.concatenate([first, second], axis=0).astype(low)
        own_copies.append(keep(chip, full.at[z, y, x, :, lanes(core, half, 0, half)]))

    att_a = (full_att, HALF_ATT, 0, 512, 4)
    att_b = (full_att, HALF_ATT, 512, 512, 4)
    out_c = (full_out, HALF_OUT, 0, 512, 4)
    down_a = (full_down, HALF_DOWN, 0, 256, 18)
    down_b = (full_down, HALF_DOWN, 256, 256, 18)
    joint_first = (full_joint, HALF_JOINT, 0, 1152, 4)
    joint_rest = [
        [(full_joint, HALF_JOINT, 1152 * turn + 384 * third, 384, 4) for third in range(3)]
        for turn in range(1, 4)
    ]

    def shape(array, zs, ys, xs):
        ref, half, begin, width, _ = array
        return ref.at[zs, ys, xs, :, lanes(core, half, begin, width)]

    def direct(source, array, axis):
        return [
            links.send(source, shape(array, z, y, x), place.near(axis, step)[1]) for step in (1, 3, 2)
        ]

    chip_block(swaps[0], att, got_att, low_att, full_att, HALF_ATT)
    chip_block(swaps[1], out, got_out, low_out, full_out, HALF_OUT)
    first = direct(low_att.at[:, 0:512], att_a, "x")
    first += direct(low_att.at[:, 512:1024], att_b, "x")
    first += direct(low_out, out_c, "y")
    gain_swap.wait_recv()
    x_gains[x] = core_gains[0] + core_gains[1]
    gain_moves = [
        links.send(x_gains.at[x], x_gains.at[x], place.near("x", step)[1]) for step in (1, 2, 3)
    ]
    pad_down[...] = jnp.zeros_like(pad_down)
    pad_down[0:DOWN_ROWS, :] = down[...]
    for part in range(2):
        send_down[part] = pad_down[:, part * 512 : part * 512 + 512].astype(low)
    down_moves = []
    for step in range(4):
        spot = lax.rem(x + step, 4)
        for flip in range(2):
            if step or flip:
                target_core = lax.rem(core + flip, 2)
                down_moves.append(
                    links.send(
                        send_down.at[target_core], got_down.at[seat], place.at(x=spot, core=target_core)
                    )
                )
    got_down[pl.ds(seat, 1)] = send_down[pl.ds(core, 1)]
    chip_block(swaps[2], joint, got_joint, low_joint, full_joint, HALF_JOINT)

    def slab_zy(array, spot, half):
        return shape(array, z, spot, half)

    def slab_yz(array, spot, half):
        return shape(array, spot, y, half)

    def slab_xz(array, spot, half):
        return shape(array, spot, half, x)

    def slab_z(array, spot, half):
        return shape(array, spot, half, ALL)

    def slab_y(array, spot, half):
        return shape(array, half, spot, ALL)

    def slab_x(array, spot, half):
        return shape(array, half, ALL, spot)

    def plans(arrays):
        ones = ((slab_zy, "y", True), (slab_yz, "z", True), (slab_xz, "z", False))
        twos = ((slab_z, "z", False), (slab_y, "y", False), (slab_x, "x", False))
        return (
            [(array,) + one for array, one in zip(arrays, ones)],
            [(array,) + two for array, two in zip(arrays, twos)],
        )

    stages = [plans(arrays) for arrays in [(att_a, att_b, out_c), (down_a, down_b, joint_first)] + joint_rest]

    def halves(inner, array):
        size = array[4] // 2 if inner else 2
        return pl.ds(0, size), pl.ds(size, size)

    def hand_over(ref, handed):
        handed.append(links.send(ref, ref, place.sibling))

    def ring_start(plans):
        moves = []
        for array, slab, axis, inner in plans:
            held = slab(array, getattr(place, axis), ALL)
            moves.append(
                [links.send(held, held, place.near(axis, 1)[1]), links.send(held, held, place.near(axis, -1)[1])]
            )
        return moves

    def ring_turn(plans, moves, handed):
        later = []
        for (array, slab, axis, inner), (upward, downward) in zip(plans, moves):
            forth, forth_device = place.near(axis, 1)
            back, back_device = place.near(axis, -1)
            one, two = halves(inner, array)
            upward.wait_recv()
            held = slab(array, back, one)
            pair = [links.send(held, held, forth_device)]
            downward.wait_recv()
            held = slab(array, forth, two)
            pair.append(links.send(held, held, back_device))
            later.append(pair)
        for array, slab, axis, inner in plans:
            hand_over(slab(array, place.near(axis, -1)[0], ALL), handed)
            hand_over(slab(array, place.near(axis, 1)[0], ALL), handed)
        return later

    def ring_close(plans, later, handed):
        for (array, slab, axis, inner), pair in zip(plans, later):
            far, _ = place.near(axis, 2)
            for move, half in zip(pair, halves(inner, array)):
                move.wait_recv()
                hand_over(slab(array, far, half), handed)

    handed = [[] for _ in stages]
    ring, second = {}, {}

    def begin_inner(spot):
        ring[spot] = ring_start(stages[spot][0])

    def turn_inner(spot):
        ring[spot] = ring_turn(stages[spot][0], ring[spot], handed[spot])
        for array, slab, axis, inner in stages[spot][0]:
            hand_over(slab(array, getattr(place, axis), ALL), handed[spot])

    def end_inner(spot):
        ring_close(stages[spot][0], ring[spot], handed[spot])

    def begin_stage(spot):
        second[spot] = ring_start(stages[spot][1])

    def turn_stage(spot):
        second[spot] = ring_turn(stages[spot][1], second[spot], handed[spot])

    def end_stage(spot):
        ring_close(stages[spot][1], second[spot], handed[spot])
        for move in handed[spot]:
            move.wait_recv()

    for copy in own_copies[:2]:
        copy.wait()
    for move in first:
        move.wait_recv()
    begin_inner(0)
    first = direct(low_joint.at[:, 0:1152], joint_first, "y")
    for arrays in joint_rest:
        for array, axis in zip(arrays, "xxy"):
            first += direct(low_joint.at[:, array[2] : array[2] + 384], array, axis)
    for move in gain_moves:
        move.wait_recv()
    all_gains[z, y] = x_gains[0] + x_gains[1] + x_gains[2] + x_gains[3]
    gain_moves = [
        links.send(all_gains.at[z, y], all_gains.at[z, y], place.near("y", step)[1])
        for step in (1, 2, 3)
    ]
    turn_inner(0)
    keep(cotangent.at[:, lanes(core, 512, 0, 512)], down_pair.at[0])
    pair_moves = [
        links.send(cotangent.at[:, lanes(other, 512, 0, 512)], down_pair.at[1], place.sibling)
    ]
    for move in down_moves:
        move.wait_recv()
    for spot in range(8):
        rows_down[spot * DOWN_ROWS : spot * DOWN_ROWS + DOWN_ROWS, :] = got_down[spot].astype(wide)[
            0:DOWN_ROWS
        ]
    low_down[...] = rows_down[...].reshape(18, 16, 512).astype(low)
    own_copies.append(keep(low_down, full_down.at[z, y, :, :, lanes(core, 512, 0, 512)]))
    end_inner(0)
    begin_stage(0)
    for move in gain_moves:
        move.wait_recv()
    gain_moves = [
        links.send(all_gains.at[z], all_gains.at[z], place.near("z", step)[1]) for step in (1, 2, 3)
    ]
    for copy in own_copies[2:]:
        copy.wait()
    for move in first:
        move.wait_recv()
    begin_inner(1)
    for move in gain_moves:
        move.wait_recv()

    flat = lax.broadcasted_iota(jnp.int32, (128, 2176), 1)
    owner = lax.broadcasted_iota(jnp.int32, (128, 2176), 0)
    holds = (flat >= 17 * owner) & (flat < 17 * owner + 17)
    spread = over_rows(
        all_gains[...].reshape(128, 128).astype(low), jnp.where(holds, 1.0, 0.0).astype(low)
    )
    offset = jnp.sum(jnp.where(holds, flat - 17 * owner, 0), axis=0, keepdims=True)
    ordered = jnp.sum(jnp.where(owner == offset, spread, 0.0), axis=0, keepdims=True)
    gain_attn[...] = ordered[:, 0:D]
    gain_ffn[...] = ordered[:, D : 2 * D]
    heads = ordered[:, 2 * D : 2 * D + 128]
    turned_heads = pltpu.roll(heads, HD, 1)
    left = lax.broadcasted_iota(jnp.int32, (1, 128), 1) < HD
    gain_query[...] = jnp.where(left, heads, turned_heads)
    gain_key[...] = jnp.where(left, turned_heads, heads)

    @pl.loop(0, 8)
    def _(turn):
        rows = pl.ds(pl.multiple_of(turn * 32, 32), 32)
        block = tokens[rows, :].astype(wide)
        inverse = lax.rsqrt(jnp.mean(block * block, axis=1, keepdims=True) + EPS)
        norm[rows, :] = (block * inverse * gain_attn[...]).astype(low)

    def flip_into(source, target):
        @pl.loop(0, 8)
        def _(turn):
            cols = pl.ds(pl.multiple_of(turn * 128, 128), 128)
            target[cols, :] = source[:, cols].T

    def share(source, pair):
        keep(source, pair.at[0])
        pair_moves.append(links.send(source, pair.at[1], place.sibling))

    flip_into(norm, norm_t)
    share(norm_t, norm_pair)
    turn_inner(1)
    turn_stage(0)
    end_inner(1)
    begin_stage(1)
    for spot in (2, 3, 4):
        begin_inner(spot)
    end_stage(0)
    keep(full_att, kept_att)
    keep(full_out, kept_out)

    @pl.loop(0, 4)
    def _(turn):
        cols = pl.ds(pl.multiple_of(turn * 512, 512), 512)
        raw[:, cols] = plain(norm[...], full_att[:, :, :, :, cols].reshape(D, 512))

    attention_heads(raw, cosine, signed_sine, segments, gain_query, gain_key, query, key, value, attended)
    for source, target in ((raw, raw_out), (query, query_out), (key, key_out), (value, value_out)):
        keep(source, target)
    turn_stage(1)
    for spot in (2, 3, 4):
        turn_inner(spot)

    @pl.loop(0, 2)
    def _(turn):
        cols = pl.ds(pl.multiple_of(turn * 512, 512), 512)
        block = plain(attended[...], full_out[:, :, :, :, cols].reshape(D, 512))
        middle[:, cols] = tokens[:, cols].astype(wide) + block

    @pl.loop(0, 8)
    def _(turn):
        rows = pl.ds(pl.multiple_of(turn * 32, 32), 32)
        block = middle[rows, :]
        middle_sum[rows, :] = block
        inverse = lax.rsqrt(jnp.mean(block * block, axis=1, keepdims=True) + EPS)
        mid[rows, :] = (block * inverse * gain_ffn[...]).astype(low)

    flip_into(attended, attended_t)
    share(attended_t, attended_pair)
    flip_into(mid, mid_t)
    share(mid_t, mid_pair)
    grad_mid[...] = jnp.zeros_like(grad_mid)

    used = {}

    def feed_forward(turn, between):
        slot = turn % 2
        if turn >= 2:
            for copy in used[turn - 2][:2]:
                copy.wait()
                own_copies.append(copy)
            for copy in used[turn - 2][2:]:
                copy.wait_send()
                links.gone.append(copy)
        cols = pl.ds(1152 * turn, 1152)

        def joint_cols(part):
            return full_joint[:, :, :, :, part * FF + 1152 * turn : part * FF + 1152 * turn + 1152].reshape(
                D, 1152
            )

        gate[...] = plain(mid[...], joint_cols(0))
        up[...] = plain(mid[...], joint_cols(1))
        grad_hidden[...] = near_rows(cotangent[...], full_down[turn].reshape(1152, D))

        @pl.loop(0, 16)
        def _(piece):
            rows = pl.ds(pl.multiple_of(piece * 16, 16), 16)
            gate_rows, up_rows, grad_rows = gate[rows, :], up[rows, :], grad_hidden[rows, :]
            sigmoid = 0.5 + 0.5 * jnp.tanh(0.5 * gate_rows)
            swish = gate_rows * sigmoid
            hidden[rows, :] = (swish * up_rows).astype(low)
            slope = sigmoid * (1.0 + gate_rows * (1.0 - sigmoid))
            grad_joint[slot, 0, rows, :] = (grad_rows * up_rows * slope).astype(low)
            grad_joint[slot, 1, rows, :] = (grad_rows * swish).astype(low)

        for begin in range(0, 1152, 128):
            hidden_t[slot, begin : begin + 128, :] = hidden[:, begin : begin + 128].T
        used[turn] = [
            keep(hidden_t.at[slot], hidden_pair.at[0, cols]),
            keep(grad_joint.at[slot, core], joint_pair.at[0, :, cols]),
            links.send(hidden_t.at[slot], hidden_pair.at[1, cols], place.sibling),
            links.send(grad_joint.at[slot, other], joint_pair.at[1, :, cols], place.sibling),
        ]
        pair_moves.extend(used[turn][2:])
        if between is not None:
            between()
        middle_sum[...] += plain(hidden[...], full_down[turn].reshape(1152, D))
        for part in range(2):
            grad_mid[...] += near_rows(grad_joint[slot, part], joint_cols(part))

    def open_four():
        turn_stage(2)
        end_inner(4)
        begin_stage(4)

    for spot in (2, 3):
        end_inner(spot)
        begin_stage(spot)
    end_stage(1)
    feed_forward(0, open_four)
    end_stage(2)
    feed_forward(1, lambda: turn_stage(3))
    end_stage(3)
    feed_forward(2, lambda: turn_stage(4))
    end_stage(4)
    feed_forward(3, None)
    ffn_gains[...] = jnp.zeros_like(ffn_gains)

    @pl.loop(0, 8)
    def _(turn):
        rows = pl.ds(pl.multiple_of(turn * 32, 32), 32)
        block = middle[rows, :]
        inverse = lax.rsqrt(jnp.mean(block * block, axis=1, keepdims=True) + EPS)
        hat = block * inverse
        grad = grad_mid[rows, :]
        ffn_gains[...] += jnp.sum(grad * hat, axis=0, keepdims=True)
        grad = grad * gain_ffn[...]
        inner = jnp.mean(grad * hat, axis=1, keepdims=True)
        grad_middle[rows, :] = inverse * (grad - hat * inner) + cotangent[rows, :].astype(wide)
        result[rows, :] = middle_sum[rows, :].astype(low)

    for move in pair_moves:
        move.wait_recv()
    for copy in locals_:
        if not any((copy is done for done in own_copies)):
            copy.wait()
    links.finish()


def gather_all(att, out, joint, down, gains, tokens, cotangent, cosine, signed_sine, segments):
    any_space = pl.BlockSpec(memory_space=pl.ANY)
    vmem = pl.BlockSpec(memory_space=pltpu.VMEM)
    low, wide = jnp.bfloat16, jnp.float32
    outputs = [
        ((4, 4, 4, 16, 2 * HALF_ATT), low, any_space),
        ((4, 4, 4, 16, 2 * HALF_OUT), low, any_space),
        ((2, FF, 256), low, any_space),
        ((2, 256, FF), low, any_space),
        ((2, D, 256), low, any_space),
        ((2, D, 256), low, any_space),
        ((2, D, 256), low, any_space),
        ((2, 256, 512), low, any_space),
        ((256, 2048), wide, any_space),
        ((256, 1024), low, any_space),
        ((256, 512), low, any_space),
        ((256, 512), low, any_space),
        ((256, D), low, vmem),
        ((256, D), wide, vmem),
        ((1, D), wide, vmem),
        ((1, D), wide, vmem),
        ((1, 128), wide, vmem),
        ((1, 128), wide, vmem),
    ]
    scratch = [
        ((256, 2048), wide),
        ((256, 1024), low),
        ((256, 512), low),
        ((256, 512), low),
        ((4, 4, 4, 16, 2 * HALF_ATT), low),
        ((4, 4, 4, 16, 2 * HALF_OUT), low),
        ((4, 4, 4, 16, 2 * HALF_JOINT), low),
        ((4, 4, 18, 16, 2 * HALF_DOWN), low),
        ((8, HALF_ATT), wide),
        ((8, HALF_OUT), wide),
        ((8, HALF_JOINT), wide),
        ((16, HALF_ATT), low),
        ((16, HALF_OUT), low),
        ((16, HALF_JOINT), low),
        ((48, 2 * HALF_DOWN), wide),
        ((2, 48, HALF_DOWN), low),
        ((8, 48, HALF_DOWN), low),
        ((288, HALF_DOWN), wide),
        ((18, 16, HALF_DOWN), low),
        ((2, 8, 128), wide),
        ((4, 8, 128), wide),
        ((4, 4, 8, 128), wide),
        ((1, D), wide),
        ((1, 128), wide),
        ((256, D), low),
        ((256, D), low),
        ((256, D), low),
        ((D, 256), low),
        ((D, 256), low),
        ((D, 256), low),
        ((256, D), wide),
        ((256, D), wide),
        ((256, D), wide),
        ((256, 1152), wide),
        ((256, 1152), wide),
        ((256, 1152), wide),
        ((256, 1152), low),
        ((2, 1152, 256), low),
        ((2, 2, 256, 1152), low),
    ]
    operands = (att, out, joint, down, gains, tokens, cotangent, cosine, signed_sine, segments)
    return pl.pallas_call(
        gather_kernel,
        out_shape=tuple((jax.ShapeDtypeStruct(shape, kind) for shape, kind, _ in outputs)),
        in_specs=[vmem] * len(operands),
        out_specs=tuple((spec for _, _, spec in outputs)),
        scratch_shapes=[pltpu.VMEM(shape, kind) for shape, kind in scratch]
        + [
            pltpu.SemaphoreType.DMA((GATHER_COPIES,)),
            pltpu.SemaphoreType.DMA((GATHER_COPIES,)),
            pltpu.SemaphoreType.DMA((32,)),
        ],
        compiler_params=pltpu.CompilerParams(
            collective_id=0, has_side_effects=True, vmem_limit_bytes=60 * 1024 * 1024
        ),
        name="gather_weights",
    )(*operands)


class Product:
    def __init__(self, left, right, low, width, axis, buffers):
        self.left, self.right, self.low, self.width, self.axis = left, right, low, width, axis
        (
            self.far, self.side, self.p, self.m, self.pp, self.mm,
            self.p2, self.m2, self.pp2, self.mm2, self.third,
        ) = buffers
        self.inner = self.p.shape[1]
        self.chunk = min(width, 1152)

    def rows(self, token, spot, half):
        two = pl.ds(2 * half, 2)
        if self.axis == "z":
            block = self.left[token, spot, two]
        elif self.axis == "y":
            block = self.left[token, two, spot]
        else:
            block = self.left[token, two, :, spot]
        return block.reshape(2 * self.inner * 16, 256)

    def fill(self, spot, half, sink):
        first, second = self.rows(0, spot, half), self.rows(1, spot, half)

        def step(begin):
            source = pl.ds(pl.multiple_of(self.low + begin, 128), self.chunk)
            value = plain(first, self.right[0, :, source]) + plain(second, self.right[1, :, source])
            sink(
                pl.ds(pl.multiple_of(begin, 128), self.chunk),
                value.reshape(2, self.inner, 16, self.chunk),
            )

        if self.width == self.chunk:
            step(0)
        else:
            @pl.loop(0, self.width // self.chunk)
            def _(turn):
                step(turn * self.chunk)


def scatter_kernel(
    grad_middle, gain_attn, gain_query, gain_key, ffn_gains, *rest,
):
    sources, rest = rest[:FETCHED], rest[FETCHED:]
    grad_att, grad_out, grad_joint, grad_down, grad_gains, grad_squares, rows_out = rest[:7]
    scratch = list(rest[7:])

    def take(count):
        taken = scratch[:count]
        del scratch[:count]
        return taken

    buffers = [take(11) for _ in range(9)]
    chip_joint, chip_att, chip_out = take(3)
    rows_down, cut_down, got_down = take(3)
    gain_slots, square_slots = take(4), take(3)
    pad_down, own_gains, head_gains, grad_attended, grad_mixed = take(5)
    mixed_pair, mixed_away, branch_pair, branch_away = take(4)
    grad_rows, grad_key = take(2)
    fetched = take(FETCHED)
    send_sems, recv_sems, own_sems = take(3)
    fetches = [
        pltpu.make_async_copy(source, target, own_sems.at[spot])
        for spot, (source, target) in enumerate(zip(sources, fetched))
    ]
    for fetch in fetches:
        fetch.start()
    (
        mid_t, grad_joint_in, hidden_t, down_in, attended_t, weight_out, raw, query, key, value,
        cosine, signed_sine, segments, norm_t, weight_att, tokens,
    ) = fetched
    place = Place()
    core, z, y, x = place.core, place.z, place.y, place.x
    other = 1 - core
    links = Links(send_sems, recv_sems)
    place.greet()
    wide, low = jnp.float32, jnp.bfloat16
    one, two = pl.ds(0, 2), pl.ds(2, 2)

    def swap(buffer, value):
        buffer[core] = value
        return [links.send(buffer.at[core], buffer.at[core], place.sibling)]

    def deal(buffer, axis, value):
        spot = getattr(place, axis)
        buffer[spot] = value
        return [
            links.send(buffer.at[spot], buffer.at[spot], place.near(axis, step)[1])
            for step in (1, 2, 3)
        ]

    def total(moves, buffer, count):
        for move in moves:
            move.wait_recv()
        value = buffer[0]
        for spot in range(1, count):
            value = value + buffer[spot]
        return value

    def start_far(job):
        far, _ = place.near(job.axis, 2)
        forth, back = place.near(job.axis, 1)[1], place.near(job.axis, -1)[1]
        moves = []
        for half, device, target in ((0, forth, job.p), (1, back, job.m)):
            span = pl.ds(2 * half, 2)

            def sink(cols, block):
                job.far[span, :, :, cols] = block.astype(low)

            job.fill(far, half, sink)
            moves.append(links.send(job.far.at[span], target, device))
        return moves

    def start_sides(job):
        forth, forth_device = place.near(job.axis, 1)
        back, back_device = place.near(job.axis, -1)

        def sink_forth(cols, block):
            job.side[two, :, :, cols] = block.astype(low)

        def sink_back(cols, block):
            job.side[one, :, :, cols] = block.astype(low)

        job.fill(forth, 1, sink_forth)
        moves = [links.send(job.side.at[two], job.pp.at[two], forth_device)]
        job.fill(back, 0, sink_back)
        moves.append(links.send(job.side.at[one], job.mm.at[one], back_device))
        return moves

    def turn_first(job, early):
        forth, forth_device = place.near(job.axis, 1)
        back, back_device = place.near(job.axis, -1)

        def sink_forth(cols, block):
            job.p[:, :, :, cols] = (job.p[:, :, :, cols].astype(wide) + block).astype(low)

        def sink_back(cols, block):
            job.m[:, :, :, cols] = (job.m[:, :, :, cols].astype(wide) + block).astype(low)

        early[0].wait_recv()
        job.fill(forth, 0, sink_forth)
        moves = [links.send(job.p, job.pp.at[one], forth_device)]
        early[1].wait_recv()
        job.fill(back, 1, sink_back)
        moves.append(links.send(job.m, job.mm.at[two], back_device))
        return moves

    def close_first(job, moves):
        for move in moves:
            move.wait_recv()
        spot = getattr(place, job.axis)
        for half in range(2):
            span = pl.ds(2 * half, 2)

            def sink(cols, block):
                got = job.pp[span, :, :, cols].astype(wide) + job.mm[span, :, :, cols].astype(wide)
                job.pp[span, :, :, cols] = (got + block).astype(low)

            job.fill(spot, half, sink)

    def start_second(job, axis):
        half = job.inner // 2
        first, last = pl.ds(0, half), pl.ds(half, half)
        forth, forth_device = place.near(axis, 1)
        back, back_device = place.near(axis, -1)
        far, _ = place.near(axis, 2)
        early = [
            links.send(job.pp.at[far, first], job.p2, forth_device),
            links.send(job.pp.at[far, last], job.m2, back_device),
        ]
        later = [
            links.send(job.pp.at[forth, last], job.pp2.at[last], forth_device),
            links.send(job.pp.at[back, first], job.mm2.at[first], back_device),
        ]
        return early, later

    def turn_second(job, axis, early):
        half = job.inner // 2
        first, last = pl.ds(0, half), pl.ds(half, half)
        forth, forth_device = place.near(axis, 1)
        back, back_device = place.near(axis, -1)
        early[0].wait_recv()

        @pl.loop(0, half)
        def _(i):
            job.p2[i] = (job.p2[i].astype(wide) + job.pp[forth, i].astype(wide)).astype(low)

        moves = [links.send(job.p2, job.pp2.at[first], forth_device)]
        early[1].wait_recv()

        @pl.loop(0, half)
        def _(i):
            job.m2[i] = (job.m2[i].astype(wide) + job.pp[back, i + half].astype(wide)).astype(low)

        moves.append(links.send(job.m2, job.mm2.at[last], back_device))
        return moves

    def close_second(job, axis, moves):
        for move in moves:
            move.wait_recv()
        spot = getattr(place, axis)

        @pl.loop(0, job.inner)
        def _(i):
            value = job.pp[spot, i].astype(wide) + job.pp2[i].astype(wide) + job.mm2[i].astype(wide)
            job.pp2[i] = value.astype(low)

    def hand_out(job, axis):
        return [
            links.send(
                job.pp2.at[place.near(axis, step)[0]], job.third.at[step - 1], place.near(axis, step)[1]
            )
            for step in (1, 2, 3)
        ]

    swaps = []

    def finish_chip(job, axis, moves, chip, whole, half, squares):
        for move in moves:
            move.wait_recv()
        value = job.pp2[getattr(place, axis)].astype(wide)
        for step in range(3):
            value = value + job.third[step].astype(wide)
        chip[:, job.low : job.low + job.width] = value
        cols = lanes(core, half, job.low, job.width)
        swaps.append(
            links.send(
                chip.at[pl.ds(pl.multiple_of(8 * other, 8), 8), pl.ds(job.low, job.width)],
                whole.at[:, cols],
                place.sibling,
            )
        )
        whole[:, cols] = chip[
            pl.ds(pl.multiple_of(8 * core, 8), 8), job.low : job.low + job.width
        ]
        for begin in range(job.low, job.low + job.width, 128):
            for row in (0, 8):
                piece = chip[row : row + 8, begin : begin + 128]
                squares = squares + piece * piece
        return squares

    joint_a = Product(mid_t, grad_joint_in, 0, CUT, "z", buffers[0])
    joint_b = Product(mid_t, grad_joint_in, CUT, CUT, "y", buffers[1])
    joint_c = Product(mid_t, grad_joint_in, 2 * CUT, CUT, "x", buffers[2])
    joint_d = Product(mid_t, grad_joint_in, 3 * CUT, CUT, "x", buffers[3])
    down_a = Product(hidden_t, down_in, 0, 256, "z", buffers[4])
    down_b = Product(hidden_t, down_in, 256, 256, "y", buffers[5])
    att_a = Product(norm_t, mixed_pair, 0, 512, "z", buffers[6])
    att_b = Product(norm_t, mixed_pair, 512, 512, "y", buffers[7])
    out_c = Product(attended_t, branch_pair, 0, 512, "x", buffers[8])
    wave_one = [joint_a, joint_b, joint_c]
    wave_two = [joint_d, down_a, down_b]
    wave_three = [out_c, att_a, att_b]
    second_axis = {
        id(job): {"z": "y", "y": "z", "x": "z"}[job.axis] for job in wave_one + wave_two + wave_three
    }
    third_axis = {
        id(job): "y" if job.axis == "x" else "x" for job in wave_one + wave_two + wave_three
    }

    for begin in range(0, 1024, 256):
        branch_away[:, begin : begin + 256] = grad_middle[:, begin : begin + 256].astype(low)
    branch_pair[0] = branch_away[:, lanes(core, 512, 0, 512)]
    branch_move = links.send(
        branch_away.at[:, lanes(other, 512, 0, 512)], branch_pair.at[1], place.sibling
    )
    early, moves, later, last = {}, {}, {}, {}

    def send_far(jobs):
        for job in jobs:
            early[id(job)] = start_far(job)

    def send_sides(jobs):
        for job in jobs:
            moves[id(job)] = start_sides(job)

    def turn(jobs):
        for job in jobs:
            moves[id(job)] += turn_first(job, early[id(job)])

    def close(jobs):
        for job in jobs:
            close_first(job, moves[id(job)])
            early[id(job)], later[id(job)] = start_second(job, second_axis[id(job)])

    def turn_again(jobs):
        for job in jobs:
            later[id(job)] += turn_second(job, second_axis[id(job)], early[id(job)])

    def close_again(jobs):
        for job in jobs:
            close_second(job, second_axis[id(job)], later[id(job)])
            if job.inner == 4:
                last[id(job)] = hand_out(job, third_axis[id(job)])

    fetches[0].wait()
    fetches[1].wait()
    send_far(wave_one)
    send_sides(wave_one)
    for fetch in fetches[2:]:
        fetch.wait()

    @pl.loop(0, 4)
    def _(spot):
        cols = pl.ds(pl.multiple_of(spot * 256, 256), 256)
        grad_attended[:, cols] = near_rows(branch_away[...], weight_out[cols, :]).astype(low)

    turn(wave_one)
    send_far(wave_two)

    attention_heads_back(
        grad_attended, raw, query, key, value, cosine, signed_sine, segments, gain_query, gain_key,
        mixed_away, head_gains, grad_rows, grad_key,
    )
    mixed_pair[0] = mixed_away[:, lanes(core, 1024, 0, 1024)]
    mixed_move = links.send(
        mixed_away.at[:, lanes(other, 1024, 0, 1024)], mixed_pair.at[1], place.sibling
    )
    send_sides(wave_two)
    close(wave_one)
    branch_move.wait_recv()
    mixed_move.wait_recv()
    send_far(wave_three)
    send_sides(wave_three)
    turn(wave_two)
    turn_again(wave_one)

    @pl.loop(0, 4)
    def _(turn):
        cols = pl.ds(pl.multiple_of(turn * 256, 256), 256)
        grad_rows[:, cols] = near_rows(mixed_away[...], weight_att[cols, :])

    own_gains[...] = jnp.zeros_like(own_gains)

    @pl.loop(0, 8)
    def _(turn):
        rows = pl.ds(pl.multiple_of(turn * 32, 32), 32)
        block = tokens[rows, :].astype(wide)
        inverse = lax.rsqrt(jnp.mean(block * block, axis=1, keepdims=True) + EPS)
        hat = block * inverse
        grad = grad_rows[rows, :]
        own_gains[0:1, :] += jnp.sum(grad * hat, axis=0, keepdims=True)
        grad = grad * gain_attn[...]
        inner = jnp.mean(grad * hat, axis=1, keepdims=True)
        grad_rows[rows, :] = inverse * (grad - hat * inner) + grad_middle[rows, :]

    rows_copy = pltpu.make_async_copy(grad_rows, rows_out, own_sems.at[FETCHED])
    rows_copy.start()
    own_gains[1:2, :] = ffn_gains[...]
    own_gains[2:4, 0:128] = head_gains[...]
    gain_moves = swap(gain_slots[0], own_gains[...])
    close(wave_two)
    gain_moves = deal(gain_slots[1], "x", total(gain_moves, gain_slots[0], 2))
    turn(wave_three)
    close_again(wave_one)
    turn_again(wave_two)
    gain_moves = deal(gain_slots[2], "y", total(gain_moves, gain_slots[1], 4))
    close(wave_three)
    close_again(wave_two)
    rows_down[288:296, :] = jnp.zeros((8, 512), wide)
    rows_down[0:288, 0:256] = down_a.pp2[...].astype(wide).reshape(288, 256)
    rows_down[0:288, 256:512] = down_b.pp2[...].astype(wide).reshape(288, 256)
    for spot in range(8):
        cut_down[spot] = rows_down[spot * DOWN_ROWS : spot * DOWN_ROWS + 40, :]
    down_moves = []
    for step in range(4):
        to = lax.rem(x + step, 4)
        for flip in range(2):
            to_core = lax.rem(core + flip, 2)
            if step or flip:
                down_moves.append(
                    links.send(
                        cut_down.at[2 * to + to_core],
                        got_down.at[2 * step + flip],
                        place.at(x=to, core=to_core),
                    )
                )
    got_down[0] = cut_down[2 * x + core]
    squares = jnp.zeros((8, 128), wide)
    for job in wave_one:
        squares = finish_chip(
            job, third_axis[id(job)], last[id(job)], chip_joint, grad_joint, HALF_JOINT, squares
        )
    gain_moves = deal(gain_slots[3], "z", total(gain_moves, gain_slots[2], 4))
    turn_again(wave_three)
    squares = finish_chip(
        joint_d, third_axis[id(joint_d)], last[id(joint_d)], chip_joint, grad_joint, HALF_JOINT, squares
    )
    close_again(wave_three)
    for move in down_moves:
        move.wait_recv()
    live = lax.broadcasted_iota(jnp.int32, (40, 512), 0) < DOWN_ROWS
    for flip in range(2):
        value_down = got_down[flip]
        for step in range(1, 4):
            value_down = value_down + got_down[2 * step + flip]
        half_core = lax.rem(core + flip, 2)
        pad_down[:, lanes(half_core, 512, 0, 512)] = jnp.where(live, value_down, 0.0)
    grad_down[...] = pad_down[0:DOWN_ROWS, :]
    for row in range(0, 40, 8):
        for col in range(0, 1024, 128):
            piece = pad_down[row : row + 8, col : col + 128]
            squares = squares + piece * piece
    gain_sums = total(gain_moves, gain_slots[3], 4)
    heads = gain_sums[2:4, 0:128]
    heads = heads + pltpu.roll(heads, HD, 1)
    left = lax.broadcasted_iota(jnp.int32, (1, 128), 1) < HD
    heads = jnp.where(left, heads[0:1], heads[1:2])
    me = place.at()
    picked = jnp.zeros((1, 128), wide)
    for begin, size, part in (
        (0, D, gain_sums[0:1]), (D, D, gain_sums[1:2]), (2 * D, 128, heads)
    ):
        entry = lax.broadcasted_iota(jnp.int32, (size, 128), 0) + begin
        wanted = lax.broadcasted_iota(jnp.int32, (size, 128), 1) + 17 * me
        picked = picked + lax.dot_general(
            part, jnp.where(entry == wanted, 1.0, 0.0), (((1,), (0,)), ((), ())),
            precision=lax.Precision.HIGHEST, preferred_element_type=wide,
        )
    grad_gains[...] = picked
    gain_squares = heads * heads
    for col in range(0, D, 128):
        for part in range(2):
            piece = gain_sums[part : part + 1, col : col + 128]
            gain_squares = gain_squares + piece * piece
    once = (lax.broadcasted_iota(jnp.int32, (8, 128), 0) == 0) & (me == 0)
    squares = squares + jnp.where(once, gain_squares, 0.0)
    for job, chip, whole, half in (
        (out_c, chip_out, grad_out, HALF_OUT),
        (att_a, chip_att, grad_att, HALF_ATT),
        (att_b, chip_att, grad_att, HALF_ATT),
    ):
        squares = finish_chip(job, third_axis[id(job)], last[id(job)], chip, whole, half, squares)
    seat = 2 * x + core
    square_slots[0][seat] = squares
    square_moves = []
    for step in range(4):
        to = lax.rem(x + step, 4)
        for flip in range(2):
            if step or flip:
                square_moves.append(
                    links.send(
                        square_slots[0].at[seat],
                        square_slots[0].at[seat],
                        place.at(x=to, core=lax.rem(core + flip, 2)),
                    )
                )
    square_moves = deal(square_slots[1], "y", total(square_moves, square_slots[0], 8))
    square_moves = deal(square_slots[2], "z", total(square_moves, square_slots[1], 4))
    grad_squares[...] = total(square_moves, square_slots[2], 4)
    for move in swaps:
        move.wait_recv()
    rows_copy.wait()
    links.finish()


def scatter_all(*operands):
    vmem = pl.BlockSpec(memory_space=pltpu.VMEM)
    any_space = pl.BlockSpec(memory_space=pl.ANY)
    sources = operands[len(operands) - FETCHED :]
    low, wide = jnp.bfloat16, jnp.float32

    def ring_buffers(inner, width):
        tail = (16, width)
        half, whole = (2, inner) + tail, (4, inner) + tail
        shapes = (whole, whole, half, half, whole, whole)
        shapes += ((inner // 2,) + tail, (inner // 2,) + tail, (inner,) + tail, (inner,) + tail)
        shapes += ((3,) + tail,)
        return [pltpu.VMEM(shape, low) for shape in shapes]

    scratch = []
    for inner, width in ((4, CUT),) * 4 + ((18, 256),) * 2 + ((4, 512),) * 3:
        scratch += ring_buffers(inner, width)
    scratch += [pltpu.VMEM((16, width), wide) for width in (HALF_JOINT, HALF_ATT, HALF_OUT)]
    scratch += [
        pltpu.VMEM((296, 512), wide),
        pltpu.VMEM((8, 40, 512), wide),
        pltpu.VMEM((8, 40, 512), wide),
    ]
    scratch += [pltpu.VMEM((count, 8, 1024), wide) for count in (2, 4, 4, 4)]
    scratch += [pltpu.VMEM((count, 8, 128), wide) for count in (8, 4, 4)]
    scratch += [
        pltpu.VMEM((40, 1024), wide),
        pltpu.VMEM((8, 1024), wide),
        pltpu.VMEM((2, 128), wide),
        pltpu.VMEM((256, 1024), low),
        pltpu.VMEM((8, 128), low),
        pltpu.VMEM((2, 256, 1024), low),
        pltpu.VMEM((256, 2048), low),
        pltpu.VMEM((2, 256, 512), low),
        pltpu.VMEM((256, 1024), low),
        pltpu.VMEM((256, 1024), wide),
        pltpu.VMEM((256, 512), wide),
    ]
    scratch += [pltpu.VMEM(source.shape, source.dtype) for source in sources]
    scratch += [
        pltpu.SemaphoreType.DMA((SCATTER_COPIES,)),
        pltpu.SemaphoreType.DMA((SCATTER_COPIES,)),
        pltpu.SemaphoreType.DMA((FETCHED + 1,)),
    ]
    return pl.pallas_call(
        scatter_kernel,
        out_shape=(
            jax.ShapeDtypeStruct((8, 2 * HALF_ATT), wide),
            jax.ShapeDtypeStruct((8, 2 * HALF_OUT), wide),
            jax.ShapeDtypeStruct((8, 2 * HALF_JOINT), wide),
            jax.ShapeDtypeStruct((DOWN_ROWS, D), wide),
            jax.ShapeDtypeStruct((1, 128), wide),
            jax.ShapeDtypeStruct((8, 128), wide),
            jax.ShapeDtypeStruct((256, D), wide),
        ),
        in_specs=[vmem] * (len(operands) - FETCHED) + [any_space] * FETCHED,
        out_specs=(vmem,) * 6 + (any_space,),
        scratch_shapes=scratch,
        compiler_params=pltpu.CompilerParams(
            collective_id=1, has_side_effects=True, vmem_limit_bytes=60 * 1024 * 1024
        ),
        name="scatter_gradients",
    )(*operands)


def update_kernel(clip_limit, rates, decays, *refs):
    count = len(rates)
    squares, refs = refs[0], refs[1:]
    operands, refs = refs[: 4 * count], refs[4 * count :]
    moved, refs = refs[:2], refs[2:]
    norm_out, outs, refs = refs[0], refs[1 : 3 * count + 1], refs[3 * count + 1 :]
    targets, held, sems = refs[:2], refs[2:-1], refs[-1]
    copies = [
        pltpu.make_async_copy(source, target, sems.at[spot])
        for spot, (source, target) in enumerate(zip(operands + moved, held + targets))
    ]
    for copy in copies:
        copy.start()
    grads, weights, firsts, seconds = (held[k * count : k * count + count] for k in range(4))
    norm = jnp.sqrt(jnp.sum(squares[...], keepdims=True))
    norm_out[...] = norm
    factor = clip_limit / jnp.maximum(norm, clip_limit)
    for spot in range(count):
        for part in range(4):
            copies[part * count + spot].wait()
        width = weights[spot].shape[1]
        step = min(width, 512)
        for begin in range(0, width, step):
            cols = slice(begin, begin + step)
            updated = adam_update(
                weights[spot][:, cols],
                firsts[spot][:, cols],
                seconds[spot][:, cols],
                grads[spot][:, cols] * factor,
                rates[spot],
                decays[spot],
            )
            for part in range(3):
                outs[part * count + spot][:, cols] = updated[part]
    for copy in copies[4 * count :]:
        copy.wait()


def update_all(clip_limit, rates, decays, squares, grads, weights, firsts, seconds, moved):
    vmem = pl.BlockSpec(memory_space=pltpu.VMEM)
    any_space = pl.BlockSpec(memory_space=pl.ANY)
    fetched = (*grads, *weights, *firsts, *seconds)
    operands = (squares, *fetched, *moved)
    shapes = [jax.ShapeDtypeStruct((1, 1), jnp.float32)]
    shapes += [jax.ShapeDtypeStruct(weight.shape, jnp.float32) for weight in weights] * 3
    shapes += [jax.ShapeDtypeStruct(array.shape, array.dtype) for array in moved]
    return pl.pallas_call(
        functools.partial(update_kernel, clip_limit, rates, decays),
        out_shape=tuple(shapes),
        in_specs=[vmem] + [any_space] * (len(fetched) + len(moved)),
        out_specs=(vmem,) * len(shapes),
        scratch_shapes=[pltpu.VMEM(array.shape, array.dtype) for array in fetched]
        + [pltpu.SemaphoreType.DMA((len(fetched) + len(moved),))],
        compiler_params=pltpu.CompilerParams(vmem_limit_bytes=60 * 1024 * 1024),
        name="update_weights",
    )(*operands)

def adam_update(weight, first, second, gradient, rate, decay):
    new_first = BETA_ONE * first + (1.0 - BETA_ONE) * gradient
    new_second = SQUARE_DAMPING * second + (1.0 - SQUARE_DAMPING) * gradient * gradient
    corrected = new_first / (1.0 - BETA_ONE**STEP)
    divisor = jnp.sqrt(new_second / (1.0 - SQUARE_DAMPING**STEP)) + MOMENT_FLOOR
    return (weight - rate * (corrected / divisor + decay * weight), new_first, new_second)


def per_device(
    inputs,
    cotangent,
    segments,
    positions,
    attention_weight,
    output_weight,
    joint_projection_matrix,
    down_weight,
    gains,
    first_attend,
    first_output,
    first_gate_up,
    first_down,
    first_gains,
    second_attend,
    second_output,
    second_gate_up,
    second_down,
    second_gains,
):
    params = (attention_weight, output_weight, joint_projection_matrix, down_weight, gains)
    devices = lax.axis_size("fsdp")
    tokens = inputs.shape[0] * inputs.shape[2]
    rows = inputs.reshape(tokens, D)
    lane = jnp.arange(2 * HD)
    exponent = -(lane % (HD // 2)).astype(jnp.float32) * 2.0 / HD
    phases = positions.reshape(tokens, 1).astype(jnp.float32) * THETA**exponent
    cosine = jnp.cos(phases)
    signed_sine = jnp.sin(phases) * jnp.where(lane % HD < HD // 2, -1.0, 1.0)
    segments = segments[:, 0]
    (
        low_att, low_out, hidden_pair, joint_pair, norm_pair, attended_pair, mid_pair, down_pair,
        raw, query, key, value, result, grad_middle, ffn_gains, gain_attn, gain_query, gain_key,
    ) = gather_all(
        *params[:4], gains.reshape(1, -1), rows, cotangent.reshape(tokens, D), cosine, signed_sine, segments
    )
    *reduced, square_sums, grad_rows = scatter_all(
        grad_middle,
        gain_attn,
        gain_query,
        gain_key,
        ffn_gains,
        mid_pair.reshape(2, 4, 4, 4, 16, tokens),
        joint_pair,
        hidden_pair.reshape(2, 4, 4, 18, 16, tokens),
        down_pair,
        attended_pair.reshape(2, 4, 4, 4, 16, tokens),
        low_out.reshape(D, 2 * HALF_OUT),
        raw,
        query,
        key,
        value,
        cosine,
        signed_sine,
        segments,
        norm_pair.reshape(2, 4, 4, 4, 16, tokens),
        low_att.reshape(D, 2 * HALF_ATT),
        rows,
    )
    token_count = inputs.shape[0] * inputs.shape[1] * inputs.shape[2] * devices
    param_count = sum((weight.size for weight in params)) * devices
    clip_limit = CLIP_COEF * math.sqrt(token_count * param_count)
    step_rates = (
        0.8 / math.sqrt(D),
        0.8 / math.sqrt(H * HD // 16),
        0.8 / math.sqrt(D),
        0.8 / math.sqrt(FF),
        GAIN_RATE,
    )
    decays = (DECAY, DECAY, DECAY, DECAY, 0.0)
    firsts = (first_attend, first_output, first_gate_up, first_down, first_gains)
    seconds = (second_attend, second_output, second_gate_up, second_down, second_gains)
    reduced[4] = reduced[4][:, : gains.shape[0]]

    def flat_rows(arrays):
        return arrays[:4] + (arrays[4].reshape(1, -1),)

    grad_norm, *updated, result, grad_rows = update_all(
        clip_limit, step_rates, decays, square_sums, reduced,
        flat_rows(params), flat_rows(firsts), flat_rows(seconds), (result, grad_rows),
    )
    grad_norm = grad_norm.reshape(())
    for slot in (4, 9, 14):
        updated[slot] = updated[slot].reshape(-1)
    result = result.reshape(inputs.shape)
    grad_inputs = grad_rows.reshape(inputs.shape)
    return (
        result,
        grad_inputs,
        grad_norm,
        *updated,
    )


def solution(mesh):
    in_specs = (
        P(None, "fsdp", None, None),
        P(None, "fsdp", None, None),
        P(None, "fsdp", None),
        P(None, "fsdp", None),
        P("fsdp", None),
        P("fsdp", None),
        P("fsdp", None),
        P("fsdp", None),
        P("fsdp"),
        P("fsdp", None),
        P("fsdp", None),
        P("fsdp", None),
        P("fsdp", None),
        P("fsdp"),
        P("fsdp", None),
        P("fsdp", None),
        P("fsdp", None),
        P("fsdp", None),
        P("fsdp"),
    )
    out_specs = (
        P(None, "fsdp", None, None),
        P(None, "fsdp", None, None),
        P(),
        P("fsdp", None),
        P("fsdp", None),
        P("fsdp", None),
        P("fsdp", None),
        P("fsdp"),
        P("fsdp", None),
        P("fsdp", None),
        P("fsdp", None),
        P("fsdp", None),
        P("fsdp"),
        P("fsdp", None),
        P("fsdp", None),
        P("fsdp", None),
        P("fsdp", None),
        P("fsdp"),
    )
    return jax.shard_map(
        per_device, mesh=mesh, in_specs=in_specs, out_specs=out_specs, check_vma=False
    )
```
